32 devices in a mesh: gx: 2 (over y), gy: 4 (over x, core), gz: 4 (over z).
Axes of the slice: x: 2, y: 2, z: 4, core: 2. Of those that a mesh axis runs over, the one named last changes fastest.
Arguments:
- right_side: float32 [128, 64, 256], P('gz', 'gy', 'gx'), may hold values from -33 to 33
- initial: float32 [128, 64, 256], P('gz', 'gy', 'gx'), may hold values from -4 to 4
- kappa_sq: float32 [128, 64, 256], P('gz', 'gy', 'gx'), may hold values from 0.0004 to 4
Outputs:
- solution: float32 [128, 64, 256], P('gz', 'gy', 'gx')
- residual: float32 [128, 64, 256], P('gz', 'gy', 'gx')
The draws below stay inside these ranges and needn't reach their ends.
All inputs are finite; a program needn't handle non-finite values.
Results may differ from the reference program's by a relative error of at most 0.0001.
Values sent between devices are 32-bit elements; how exact they have to be, the bound alone decides.
A program may use at most 64 MiB of HBM per device.

```python
import math
import jax
import jax.numpy as jnp

CX = 128
ITERS = 2
SWEEPS = 3
NX = 256
NY = 64
NZ = 128


def parity_sign():
    index_z = jnp.arange(NZ, dtype=jnp.int32)[:, None, None]
    index_y = jnp.arange(NY, dtype=jnp.int32)[None, :, None]
    index_x = jnp.arange(NX, dtype=jnp.int32)[None, None, :]
    return (1 - 2 * ((index_z + index_y + index_x) % 2)).astype(jnp.float32)


def band_weight():
    place = jnp.arange(NX, dtype=jnp.int32) % CX
    distance = jnp.minimum(place, CX - 1 - place).astype(jnp.float32)
    return jnp.exp(-(distance / 6.0) * (distance / 6.0))[None, None, :]


def rising_scale():
    along_z = (jnp.arange(NZ, dtype=jnp.float32) / NZ)[:, None, None]
    along_y = (jnp.arange(NY, dtype=jnp.float32) / NY)[None, :, None]
    along_x = (jnp.arange(NX, dtype=jnp.float32) / NX)[None, None, :]
    return jnp.power(3.0, along_z + along_y + along_x)


def draw_right_side(key, part):
    sign_field = parity_sign()
    profile = 0.25 + 0.75 * band_weight()
    scaling = 1.2 * rising_scale()
    factor = jax.random.uniform(key, (NZ, NY, NX), jnp.float32, 0.4, 1.0)
    return jnp.clip(scaling * sign_field * profile * factor, -33.0, 33.0)


def draw_initial(key, part):
    sign_field = parity_sign()
    scaling = 4.0 / 27.0 * rising_scale()
    factor = jax.random.uniform(key, (NZ, NY, NX), jnp.float32, 0.3, 1.0)
    return jnp.clip(-sign_field * scaling * factor, -4.0, 4.0)


def draw_kappa_sq(key, part):
    weight = band_weight()
    floor_band = 0.85
    uniform_draw = jax.random.uniform(key, (NZ, NY, NX), jnp.float32)
    fraction = weight * floor_band + (1.0 - weight * floor_band) * uniform_draw
    values = 0.0004 * jnp.exp(fraction * math.log(10000.0))
    return jnp.clip(values, 0.0004, 4.0)


def setup_inputs(seed: int = 0) -> dict:
    keys = jax.random.split(jax.random.key(seed), 4)
    right_side = draw_right_side(jax.random.fold_in(keys[3], 71), 0)
    initial = draw_initial(jax.random.fold_in(keys[3], 71), 0)
    kappa_sq = draw_kappa_sq(jax.random.fold_in(keys[3], 71), 0)
    return dict(right_side=right_side, initial=initial, kappa_sq=kappa_sq)


cheb_high = 7.2
cheb_low = 0.072


def neighbours(padded):
    total = padded[2:, 1:-1, 1:-1] + padded[:-2, 1:-1, 1:-1]
    total = total + padded[1:-1, 2:, 1:-1] + padded[1:-1, :-2, 1:-1]
    total = total + padded[1:-1, 1:-1, 2:] + padded[1:-1, 1:-1, :-2]
    return total


def apply_k(values, kappa_sq):
    padded = jnp.pad(values, 1)
    return ((6.0 + kappa_sq) * values - neighbours(padded)) / 6.0


def apply_q(values, kappa_sq):
    return apply_k(apply_k(values, kappa_sq), kappa_sq)


def precondition(source, kappa_sq):
    centre = (cheb_high + cheb_low) / 2.0
    half_width = (cheb_high - cheb_low) / 2.0
    ratio_sigma = centre / half_width
    weight_old = 1.0 / ratio_sigma
    update = source / centre
    result = update
    for sweep in range(SWEEPS - 1):
        defect = source - apply_q(result, kappa_sq)
        weight_new = 1.0 / (2.0 * ratio_sigma - weight_old)
        update = weight_new * weight_old * update + (2.0 * weight_new / half_width) * defect
        result = result + update
        weight_old = weight_new
    return result


def reference(right_side, initial, kappa_sq):
    solution = initial
    residual = right_side - apply_q(initial, kappa_sq)
    precond = precondition(residual, kappa_sq)
    direction = precond
    energy = jnp.sum(residual * precond)
    for step in range(ITERS):
        applied = apply_q(direction, kappa_sq)
        step_size = energy / jnp.sum(direction * applied)
        solution = solution + step_size * direction
        residual = residual - step_size * applied
        if step + 1 < ITERS:
            precond = precondition(residual, kappa_sq)
            energy_new = jnp.sum(residual * precond)
            direction = precond + (energy_new / energy) * direction
            energy = energy_new
    return solution, residual
```

```python
import functools
import jax
import jax.numpy as jnp
from jax import lax
from jax.experimental import pallas as pl
from jax.experimental.pallas import tpu as pltpu
from jax.sharding import PartitionSpec as P

SWEEPS = 3
cheb_high = 7.2
cheb_low = 0.072
MESH = pl.DeviceIdType.MESH
AXES = ("gx", "gy", "gz")


def sweep_weights():
    centre = (cheb_high + cheb_low) / 2.0
    half_width = (cheb_high - cheb_low) / 2.0
    sigma = centre / half_width
    old = 1.0 / sigma
    weights = []
    for _ in range(SWEEPS - 1):
        new = 1.0 / (2.0 * sigma - old)
        weights.append((new * old, 2.0 * new / half_width))
        old = new
    return 1.0 / centre, weights


def kernel(sizes, shape, b_ref, x0_ref, kap_ref, x_ref, r_ref,
           v_ref, u_ref, t_ref, c_ref, r0_ref, z0_ref, a0_ref, d_ref,
           xsend, ysend, xhalo, yhalo, zhalo, part, gather_x, gather_y, gather_z,
           send_sem, recv_sem, red_send, red_recv):
    Z, Y, X = shape
    N = Z * Y
    CH = min(N, 8 * Y)
    chunks = [(i, CH) for i in range(0, N, CH)]
    me = {a: lax.axis_index(a) for a in AXES}
    inv_centre, weights = sweep_weights()
    inv36 = 1.0 / 36.0

    xhalo[...] = jnp.zeros_like(xhalo)
    yhalo[...] = jnp.zeros_like(yhalo)
    zhalo[...] = jnp.zeros_like(zhalo)

    barrier = pltpu.get_barrier_semaphore()
    count = 0
    for a in AXES:
        for k in range(1, sizes[a]):
            peer = lax.rem(me[a] + k, sizes[a])
            pl.semaphore_signal(barrier, inc=1, device_id={a: peer}, device_id_type=MESH)
            count += 1

    for ref in (v_ref, u_ref):
        ref[0:Y, :] = jnp.zeros((Y, X), jnp.float32)
        ref[Y + N:2 * Y + N, :] = jnp.zeros((Y, X), jnp.float32)
    for i, n in chunks:
        v_ref[Y + i:Y + i + n, :] = x0_ref[i:i + n, :]
        c_ref[i:i + n, :] = 6.0 + kap_ref[i:i + n, :]

    lane_y = lax.broadcasted_iota(jnp.int32, (Y, X), 1)
    half_y = lane_y // 2
    even_y = lane_y % 2 == 0
    edge_y = (lane_y == 0) | (lane_y == X - 1)
    lane_c = lax.broadcasted_iota(jnp.int32, (CH, X), 1)
    row_c = lax.broadcasted_iota(jnp.int32, (CH, X), 0) % Y
    first_x, last_x = lane_c == 0, lane_c == X - 1
    first_y, last_y = row_c == 0, row_c == Y - 1

    pl.semaphore_wait(barrier, count)

    def has(a, side):
        return me[a] > 0 if side == 0 else me[a] < sizes[a] - 1

    def halo_copy(src_ref, slot, ai, side, halo_side):
        a = AXES[ai]
        if ai == 0:
            src, halo = xsend.at[slot], xhalo
        elif ai == 1:
            src, halo = ysend.at[slot, side], yhalo
        else:
            src, halo = src_ref.at[pl.ds(Y if side == 0 else N, Y)], zhalo
        return pltpu.make_async_remote_copy(
            src_ref=src, dst_ref=halo.at[slot, halo_side],
            send_sem=send_sem.at[slot, ai, side],
            recv_sem=recv_sem.at[slot, ai, halo_side],
            device_id={a: me[a] + (2 * side - 1)}, device_id_type=MESH)

    def each_side(order, fn):
        for ai in order:
            if sizes[AXES[ai]] > 1:
                for side in (0, 1):
                    pl.when(has(AXES[ai], side))(functools.partial(fn, ai, side))

    def k_step(step, src, dst, dst_off, post, middle=None):
        slot = step % 2

        def start(ai, side):
            halo_copy(src, slot, ai, side, 1 - side).start()

        def finish(ai, side):
            halo_copy(src, slot, ai, side, side).wait_recv()
            halo_copy(src, slot, ai, side, 1 - side).wait_send()

        each_side((2,), start)
        for side, row in ((0, 0), (1, Y - 1)):
            ysend[slot, side] = src[pl.ds(Y + row, Z, stride=Y), :]
        each_side((1,), start)
        acc = jnp.zeros((Y, X), jnp.float32)
        for k in range(Z):
            v = src[Y + k * Y:2 * Y + k * Y, :]
            acc = jnp.where(half_y == k, pltpu.roll(v, (1 + 2 * k) % X, 1), acc)
        xsend[slot] = acc
        each_side((0,), start)

        for i, n in chunks:
            v = src[Y + i:Y + i + n, :]
            total = src[i:i + n, :] + src[2 * Y + i:2 * Y + i + n, :]
            total = total + jnp.where(first_x, 0.0, pltpu.roll(v, 1, 1))
            total = total + jnp.where(last_x, 0.0, pltpu.roll(v, X - 1, 1))
            total = total + jnp.where(first_y, 0.0, pltpu.roll(v, 1, 0))
            total = total + jnp.where(last_y, 0.0, pltpu.roll(v, n - 1, 0))
            dst[dst_off + i:dst_off + i + n, :] = c_ref[i:i + n, :] * v - total
        if middle is not None:
            middle()

        each_side((2, 1, 0), finish)
        for side, row in ((0, 0), (1, N - Y)):
            rows = slice(dst_off + row, dst_off + row + Y)
            dst[rows, :] = dst[rows, :] - zhalo[slot, side]
        for side, row in ((0, 0), (1, Y - 1)):
            rows = pl.ds(dst_off + row, Z, stride=Y)
            dst[rows, :] = dst[rows, :] - yhalo[slot, side]
        pairs = jnp.where(even_y, pltpu.roll(xhalo[slot, 1], X - 1, 1),
                          pltpu.roll(xhalo[slot, 0], 1, 1))
        for k in range(Z):
            rows = slice(dst_off + k * Y, dst_off + (k + 1) * Y)
            fix = jnp.where(edge_y, pltpu.roll(pairs, (X - 1 - 2 * k) % X, 1), 0.0)
            post(k * Y, dst[rows, :] - fix)

    def store_u(i, value):
        u_ref[Y + i:2 * Y + i, :] = value

    def q_step(step, post):
        k_step(step, v_ref, u_ref, Y, store_u)
        k_step(step + 1, u_ref, t_ref, 0, post)

    def post_residual(i, t):
        rows = slice(i, i + Y)
        res = b_ref[rows, :] - t * inv36
        r0_ref[rows, :] = res
        upd = res * inv_centre
        d_ref[rows, :] = upd
        v_ref[Y + i:2 * Y + i, :] = upd

    def post_sweep(source, weight_old, weight_new, i, t, sink=None):
        rows = slice(i, i + Y)
        src = source[rows, :]
        upd = weight_old * d_ref[rows, :] + weight_new * (src - t * inv36)
        d_ref[rows, :] = upd
        z = v_ref[Y + i:2 * Y + i, :] + upd
        v_ref[Y + i:2 * Y + i, :] = z
        if sink is not None:
            sink(rows, src, z)

    sums = {}

    def add(name, value):
        sums[name] = value if name not in sums else sums[name] + value

    step = 0
    q_step(step, post_residual)
    step += 2

    def sink_z0(rows, src, z):
        z0_ref[rows, :] = z
        add("e0", src * z)

    def sink_w(rows, src, z):
        add("g2", src * z)

    def sweeps(step, source, sink):
        for j, (wo, wn) in enumerate(weights):
            last = sink if j + 1 == len(weights) else None
            q_step(step, functools.partial(post_sweep, source, wo, wn, sink=last))
            step += 2
        return step

    step = sweeps(step, r0_ref, sink_z0)

    def post_applied(i, t):
        rows = slice(i, i + Y)
        a0 = t * inv36
        a0_ref[rows, :] = a0
        add("g1", z0_ref[rows, :] * a0)
        upd = a0 * inv_centre
        d_ref[rows, :] = upd
        v_ref[Y + i:2 * Y + i, :] = upd

    q_step(step, post_applied)
    step += 2
    step = sweeps(step, a0_ref, sink_w)

    def post_u(i, value):
        store_u(i, value)
        add("g3", value * value)

    k_step(step, v_ref, u_ref, Y, post_u)

    gathers = {"gx": gather_x, "gy": gather_y, "gz": gather_z}

    def red_copy(ai, k, slot):
        a = AXES[ai]
        peer = lax.rem(me[a] + k, sizes[a])
        return pltpu.make_async_remote_copy(
            src_ref=part.at[ai], dst_ref=gathers[a].at[slot],
            send_sem=red_send.at[ai, k], recv_sem=red_recv.at[ai, k],
            device_id={a: peer}, device_id_type=MESH)

    def red_start(ai, value):
        a = AXES[ai]
        part[ai] = value
        gathers[a][pl.ds(me[a], 1)] = value[None]
        for k in range(1, sizes[a]):
            red_copy(ai, k, me[a]).start()

    def red_finish(ai):
        a = AXES[ai]
        for k in range(1, sizes[a]):
            red_copy(ai, k, lax.rem(me[a] + sizes[a] - k, sizes[a])).wait_recv()
            red_copy(ai, k, me[a]).wait_send()
        total = gathers[a][0]
        for j in range(1, sizes[a]):
            total = total + gathers[a][j]
        return total

    rows8 = lax.broadcasted_iota(jnp.int32, (8, X), 0)
    mine = jnp.zeros((8, X), jnp.float32)
    for j, name in enumerate(("e0", "g1", "g2", "g3")):
        mine = jnp.where(rows8 == j, jnp.sum(sums[name], axis=0, keepdims=True), mine)
    red_start(1, mine)

    def middle():
        red_start(0, red_finish(1))

    def post_qw(i, t):
        t_ref[i:i + Y, :] = t

    k_step(step + 1, u_ref, t_ref, 0, post_qw, middle)
    red_start(2, red_finish(0))
    totals = jnp.sum(red_finish(2), axis=1, keepdims=True)
    e0, g1, g2 = totals[0:1], totals[1:2], totals[2:3]
    g3 = totals[3:4] * inv36
    alpha = e0 / g1
    e1 = e0 - 2.0 * alpha * g1 + alpha * alpha * g2
    keep = 1.0 + e1 / e0
    den = keep * keep * g1 - 2.0 * keep * alpha * g2 + alpha * alpha * g3
    alpha1 = e1 / den
    p = alpha + alpha1 * keep
    q = alpha1 * alpha
    q36 = q * inv36
    for i, n in chunks:
        rows = slice(i, i + n)
        x_ref[rows, :] = x0_ref[rows, :] + p * z0_ref[rows, :] - q * v_ref[Y + i:Y + i + n, :]
        r_ref[rows, :] = r0_ref[rows, :] - p * a0_ref[rows, :] + q36 * t_ref[rows, :]


def body(sizes, right_side, initial, kappa_sq):
    Z, Y, X = right_side.shape
    N = Z * Y
    f32 = jnp.float32
    flat = lambda a: a.reshape(N, X)
    vm = pl.BlockSpec(memory_space=pltpu.VMEM)
    big = max(sizes.values())
    out = pl.pallas_call(
        functools.partial(kernel, sizes, (Z, Y, X)),
        out_shape=[jax.ShapeDtypeStruct((N, X), f32)] * 2,
        in_specs=[vm] * 3,
        out_specs=[vm] * 2,
        scratch_shapes=[
            pltpu.VMEM((N + 2 * Y, X), f32),
            pltpu.VMEM((N + 2 * Y, X), f32),
        ] + [pltpu.VMEM((N, X), f32)] * 6 + [
            pltpu.VMEM((2, Y, X), f32),
            pltpu.VMEM((2, 2, Z, X), f32),
            pltpu.VMEM((2, 2, Y, X), f32),
            pltpu.VMEM((2, 2, Z, X), f32),
            pltpu.VMEM((2, 2, Y, X), f32),
            pltpu.VMEM((3, 8, X), f32),
        ] + [pltpu.VMEM((sizes[a], 8, X), f32) for a in AXES] + [
            pltpu.SemaphoreType.DMA((2, 3, 2)),
            pltpu.SemaphoreType.DMA((2, 3, 2)),
            pltpu.SemaphoreType.DMA((3, big)),
            pltpu.SemaphoreType.DMA((3, big)),
        ],
        compiler_params=pltpu.CompilerParams(
            collective_id=0, has_side_effects=True, vmem_limit_bytes=24 * 1024 * 1024),
        name="cg",
    )(flat(right_side), flat(initial), flat(kappa_sq))
    return tuple(o.reshape(Z, Y, X) for o in out)


def solution(mesh):
    spec = P("gz", "gy", "gx")
    sizes = {a: mesh.shape[a] for a in AXES}
    return jax.shard_map(functools.partial(body, sizes), mesh=mesh, in_specs=(spec,) * 3,
                         out_specs=(spec,) * 2, check_vma=False)
```

```python
import functools
import jax
import jax.numpy as jnp
from jax import lax
from jax.experimental import pallas as pl
from jax.experimental.pallas import tpu as pltpu
from jax.sharding import PartitionSpec as P

SWEEPS = 3
cheb_high = 7.2
cheb_low = 0.072
MESH = pl.DeviceIdType.MESH
AXES = ("gx", "gy", "gz")


def sweep_weights():
    centre = (cheb_high + cheb_low) / 2.0
    half_width = (cheb_high - cheb_low) / 2.0
    sigma = centre / half_width
    old = 1.0 / sigma
    weights = []
    for _ in range(SWEEPS - 1):
        new = 1.0 / (2.0 * sigma - old)
        weights.append((new * old, 2.0 * new / half_width))
        old = new
    return 1.0 / centre, weights


def kernel(sizes, shape, b_hbm, x0_hbm, kap_hbm, x_ref, r_ref,
           v_ref, e_ref, u_ref, t_ref, c_ref, d_ref,
           xsend, ysend, xhalo, yhalo, zhalo, sums_s, sums_v, sums_u, part,
           gather_x, gather_y, gather_z,
           send_sem, recv_sem, red_send, red_recv, in_sem):
    Z, Y, X = shape
    N = Z * Y
    me = {a: lax.axis_index(a) for a in AXES}
    inv_centre, weights = sweep_weights()
    inv36 = 1.0 / 36.0
    half = SWEEPS
    last_q = 2 * half
    zero_slot = last_q + 2

    loads = [pltpu.make_async_copy(x0_hbm, v_ref.at[0, pl.ds(Y, N)], in_sem.at[0]),
             pltpu.make_async_copy(kap_hbm, c_ref, in_sem.at[1]),
             pltpu.make_async_copy(b_hbm, e_ref.at[0], in_sem.at[2])]
    for load in loads:
        load.start()

    xhalo[...] = jnp.zeros_like(xhalo)
    yhalo[...] = jnp.zeros_like(yhalo)
    zhalo[...] = jnp.zeros_like(zhalo)

    barrier = pltpu.get_barrier_semaphore()
    count = 0
    for a in AXES:
        for k in range(1, sizes[a]):
            peer = lax.rem(me[a] + k, sizes[a])
            pl.semaphore_signal(barrier, inc=1, device_id={a: peer}, device_id_type=MESH)
            count += 1

    guard = jnp.zeros((Y, X), jnp.float32)
    for j in range(last_q + 2):
        v_ref[j, 0:Y, :] = guard
        v_ref[j, Y + N:2 * Y + N, :] = guard
    u_ref[0:Y, :] = guard
    u_ref[Y + N:2 * Y + N, :] = guard
    for k in range(Z):
        e_ref[zero_slot, k * Y:(k + 1) * Y, :] = guard
        d_ref[k * Y:(k + 1) * Y, :] = guard

    lane = lax.broadcasted_iota(jnp.int32, (Y, X), 1)
    row = lax.broadcasted_iota(jnp.int32, (Y, X), 0)
    half_lane = lane // 2
    even = lane % 2 == 0
    first_x, last_x = lane == 0, lane == X - 1
    edge_x = first_x | last_x
    first_y, last_y = row == 0, row == Y - 1

    loads[0].wait()
    loads[1].wait()
    for k in range(Z):
        rows = slice(k * Y, (k + 1) * Y)
        c_ref[rows, :] = 6.0 + c_ref[rows, :]
    loads[2].wait()
    pl.semaphore_wait(barrier, count)

    def has(a, side):
        return me[a] > 0 if side == 0 else me[a] < sizes[a] - 1

    def halo_copy(src_ref, slot, ai, side, halo_side):
        a = AXES[ai]
        if ai == 0:
            src, halo = xsend.at[slot], xhalo
        elif ai == 1:
            src, halo = ysend.at[slot, side], yhalo
        else:
            src, halo = src_ref.at[pl.ds(Y if side == 0 else N, Y)], zhalo
        return pltpu.make_async_remote_copy(
            src_ref=src, dst_ref=halo.at[slot, halo_side],
            send_sem=send_sem.at[slot, ai, side],
            recv_sem=recv_sem.at[slot, ai, halo_side],
            device_id={a: me[a] + (2 * side - 1)}, device_id_type=MESH)

    def each_side(order, fn):
        for ai in order:
            if sizes[AXES[ai]] > 1:
                for side in (0, 1):
                    pl.when(has(AXES[ai], side))(functools.partial(fn, ai, side))

    def k_step(slot, src, dst, dst_off, post, middle=None):
        def start(ai, side):
            halo_copy(src, slot, ai, side, 1 - side).start()

        def finish(ai, side):
            halo_copy(src, slot, ai, side, side).wait_recv()
            halo_copy(src, slot, ai, side, 1 - side).wait_send()

        each_side((2,), start)
        for side, first in ((0, 0), (1, Y - 1)):
            ysend[slot, side] = src[pl.ds(Y + first, Z, stride=Y), :]
        each_side((1,), start)
        acc = jnp.zeros((Y, X), jnp.float32)
        for k in range(Z):
            v = src[Y + k * Y:2 * Y + k * Y, :]
            acc = jnp.where(half_lane == k, pltpu.roll(v, (1 + 2 * k) % X, 1), acc)
        xsend[slot] = acc
        each_side((0,), start)

        for k in range(Z):
            i = Y + k * Y
            v = src[i:i + Y, :]
            total = src[i - Y:i, :] + src[i + Y:i + 2 * Y, :]
            total = total + jnp.where(first_x, 0.0, pltpu.roll(v, 1, 1))
            total = total + jnp.where(last_x, 0.0, pltpu.roll(v, X - 1, 1))
            total = total + jnp.where(first_y, 0.0, src[i - 1:i - 1 + Y, :])
            total = total + jnp.where(last_y, 0.0, src[i + 1:i + 1 + Y, :])
            dst[dst_off + k * Y:dst_off + (k + 1) * Y, :] = c_ref[k * Y:(k + 1) * Y, :] * v - total
        if middle is not None:
            middle()

        each_side((2, 1, 0), finish)
        for side, first in ((0, 0), (1, N - Y)):
            rows = slice(dst_off + first, dst_off + first + Y)
            dst[rows, :] = dst[rows, :] - zhalo[slot, side]
        for side, first in ((0, 0), (1, Y - 1)):
            rows = pl.ds(dst_off + first, Z, stride=Y)
            dst[rows, :] = dst[rows, :] - yhalo[slot, side]
        pairs = jnp.where(even, pltpu.roll(xhalo[slot, 1], X - 1, 1),
                          pltpu.roll(xhalo[slot, 0], 1, 1))
        for k in range(Z):
            rows = slice(dst_off + k * Y, dst_off + (k + 1) * Y)
            fix = jnp.where(edge_x, pltpu.roll(pairs, (X - 1 - 2 * k) % X, 1), 0.0)
            post(k, dst[rows, :] - fix)

    gathers = {"gx": gather_x, "gy": gather_y, "gz": gather_z}

    def red_copy(ai, k, slot):
        a = AXES[ai]
        peer = lax.rem(me[a] + k, sizes[a])
        return pltpu.make_async_remote_copy(
            src_ref=part.at[ai], dst_ref=gathers[a].at[slot],
            send_sem=red_send.at[ai, k], recv_sem=red_recv.at[ai, k],
            device_id={a: peer}, device_id_type=MESH)

    def red_start(ai, value):
        a = AXES[ai]
        part[ai] = value
        gathers[a][pl.ds(me[a], 1)] = value[None]
        for k in range(1, sizes[a]):
            red_copy(ai, k, me[a]).start()

    def red_finish(ai):
        a = AXES[ai]
        for k in range(1, sizes[a]):
            red_copy(ai, k, lax.rem(me[a] + sizes[a] - k, sizes[a])).wait_recv()
            red_copy(ai, k, me[a]).wait_send()
        total = gathers[a][0]
        for j in range(1, sizes[a]):
            total = total + gathers[a][j]
        return total

    def red_first():
        rows8 = lax.broadcasted_iota(jnp.int32, (8, X), 0)
        mine = jnp.zeros((8, X), jnp.float32)
        for j, value in enumerate((sums_s[half - 1], sums_v[half], sums_s[last_q - 1], sums_u[...])):
            mine = jnp.where(rows8 == j, jnp.sum(value, axis=0, keepdims=True), mine)
        red_start(1, mine)

    def red_second():
        red_start(0, red_finish(1))

    def q_body(q, carry):
        phase = lax.rem(q, half)
        sweep = jnp.minimum(phase, 1)
        source = sweep * (1 + half * (q // half)) + (1 - sweep) * zero_slot * ((q + last_q - 1) // last_q)
        sign = jnp.where((sweep == 0) & (q > 0), -1.0, 1.0).astype(jnp.float32)
        old, new, keep = jnp.float32(0.0), sign * jnp.float32(inv_centre), jnp.float32(0.0)
        for j, (wo, wn) in enumerate(weights):
            old = jnp.where(phase == j + 1, jnp.float32(wo), old)
            new = jnp.where(phase == j + 1, jnp.float32(wn), new)
            keep = jnp.where(phase == j + 1, jnp.float32(1.0), keep)
        v = v_ref.at[q]
        v_new = v_ref.at[q + 1]
        zero8 = jnp.zeros((8, X), jnp.float32)
        acc = {"u": zero8, "s": zero8, "v": zero8}

        def fold(name, value):
            for j in range(0, Y, 8):
                acc[name] = acc[name] + value[j:j + 8]

        def post_u(k, value):
            u_ref[Y + k * Y:2 * Y + k * Y, :] = value
            fold("u", value * value)

        def post_t(k, t):
            rows = slice(k * Y, (k + 1) * Y)
            vrows = slice(Y + k * Y, 2 * Y + k * Y)
            t = t * inv36
            src = e_ref[source, rows, :]
            defect = src - t
            e_ref[q + 1, rows, :] = sign * defect
            upd = old * d_ref[rows, :] + new * defect
            d_ref[rows, :] = upd
            was = v[vrows, :]
            z = keep * was + upd
            v_new[vrows, :] = z
            fold("s", src * z)
            fold("v", was * t)

        k_step(0, v, u_ref, Y, post_u)
        sums_u[...] = acc["u"]
        pl.when(q == last_q)(red_first)
        k_step(1, u_ref, t_ref, 0, post_t, lambda: pl.when(q == last_q)(red_second))
        sums_s[q] = acc["s"]
        sums_v[q] = acc["v"]
        return carry

    lax.fori_loop(0, last_q + 1, q_body, 0)

    red_start(2, red_finish(0))
    totals = jnp.sum(red_finish(2), axis=1, keepdims=True)
    e0, g1, g2 = totals[0:1], totals[1:2], totals[2:3]
    g3 = totals[3:4] * inv36
    alpha = e0 / g1
    e1 = e0 - 2.0 * alpha * g1 + alpha * alpha * g2
    keep = 1.0 + e1 / e0
    den = keep * keep * g1 - 2.0 * keep * alpha * g2 + alpha * alpha * g3
    alpha1 = e1 / den
    p = alpha + alpha1 * keep
    q = alpha1 * alpha
    for k in range(Z):
        rows = slice(k * Y, (k + 1) * Y)
        vrows = slice(Y + k * Y, 2 * Y + k * Y)
        x_ref[rows, :] = v_ref[0, vrows, :] + p * v_ref[half, vrows, :] - q * v_ref[last_q, vrows, :]
        r_ref[rows, :] = e_ref[1, rows, :] - p * e_ref[half + 1, rows, :] + q * e_ref[last_q + 1, rows, :]


def body(sizes, right_side, initial, kappa_sq):
    Z, Y, X = right_side.shape
    N = Z * Y
    f32 = jnp.float32
    flat = lambda a: a.reshape(N, X)
    vm = pl.BlockSpec(memory_space=pltpu.VMEM)
    hbm = pl.BlockSpec(memory_space=pltpu.HBM)
    big = max(sizes.values())
    count = 2 * SWEEPS + 1
    out = pl.pallas_call(
        functools.partial(kernel, sizes, (Z, Y, X)),
        out_shape=[jax.ShapeDtypeStruct((N, X), f32)] * 2,
        in_specs=[hbm] * 3,
        out_specs=[vm] * 2,
        scratch_shapes=[
            pltpu.VMEM((count + 1, N + 2 * Y, X), f32),
            pltpu.VMEM((count + 2, N, X), f32),
            pltpu.VMEM((N + 2 * Y, X), f32),
            pltpu.VMEM((N, X), f32),
            pltpu.VMEM((N, X), f32),
            pltpu.VMEM((N, X), f32),
            pltpu.VMEM((2, Y, X), f32),
            pltpu.VMEM((2, 2, Z, X), f32),
            pltpu.VMEM((2, 2, Y, X), f32),
            pltpu.VMEM((2, 2, Z, X), f32),
            pltpu.VMEM((2, 2, Y, X), f32),
            pltpu.VMEM((count, 8, X), f32),
            pltpu.VMEM((count, 8, X), f32),
            pltpu.VMEM((8, X), f32),
            pltpu.VMEM((3, 8, X), f32),
        ] + [pltpu.VMEM((sizes[a], 8, X), f32) for a in AXES] + [
            pltpu.SemaphoreType.DMA((2, 3, 2)),
            pltpu.SemaphoreType.DMA((2, 3, 2)),
            pltpu.SemaphoreType.DMA((3, big)),
            pltpu.SemaphoreType.DMA((3, big)),
            pltpu.SemaphoreType.DMA((3,)),
        ],
        compiler_params=pltpu.CompilerParams(
            collective_id=0, has_side_effects=True, vmem_limit_bytes=63 * 1024 * 1024),
        name="cg",
    )(flat(right_side), flat(initial), flat(kappa_sq))
    return tuple(o.reshape(Z, Y, X) for o in out)


def solution(mesh):
    spec = P("gz", "gy", "gx")
    sizes = {a: mesh.shape[a] for a in AXES}
    return jax.shard_map(functools.partial(body, sizes), mesh=mesh, in_specs=(spec,) * 3,
                         out_specs=(spec,) * 2, check_vma=False)
```

```python
import functools
import jax
import jax.numpy as jnp
from jax import lax
from jax.experimental import pallas as pl
from jax.experimental.pallas import tpu as pltpu
from jax.sharding import PartitionSpec as P

SWEEPS = 3
cheb_high = 7.2
cheb_low = 0.072
MESH = pl.DeviceIdType.MESH
AXES = ("gx", "gy", "gz")
DIRECTIONS = [(z, y, x) for z in (-1, 0, 1) for y in (-1, 0, 1) for x in (-1, 0, 1)
              if 1 <= abs(z) + abs(y) + abs(x) <= 2]


def group_size(sizes, axes):
    size = 1
    for a in axes:
        size *= sizes[a]
    return size


def rank(sizes, where, axes):
    index = 0
    for a in axes:
        index = index * sizes[a] + where[a]
    return index


def peers(sizes, me, axes):
    found = []
    for k in range(1, group_size(sizes, axes)):
        to, origin, left = {}, {}, k
        for a in reversed(axes):
            shift, left = left % sizes[a], left // sizes[a]
            to[a] = lax.rem(me[a] + shift, sizes[a])
            origin[a] = lax.rem(me[a] + sizes[a] - shift, sizes[a])
        found.append((to, origin))
    return found


def sweep_weights():
    centre = (cheb_high + cheb_low) / 2.0
    half_width = (cheb_high - cheb_low) / 2.0
    sigma = centre / half_width
    old = 1.0 / sigma
    weights = []
    for _ in range(SWEEPS - 1):
        new = 1.0 / (2.0 * sigma - old)
        weights.append((new * old, 2.0 * new / half_width))
        old = new
    return 1.0 / centre, weights


def kernel(sizes, phases, shape, b_hbm, x0_hbm, kap_hbm, x_ref, r_ref,
           v_ref, e_ref, u_ref, t_ref, c_ref, d_ref,
           send, xhalo, yhalo, zhalo, zyhalo, zxhalo, yxhalo, cz_ref, cy_ref, cx_ref,
           sums_s, sums_v, sums_u, part, gather_a, gather_b, gather_c,
           send_sem, recv_sem, red_send, red_recv, in_sem):
    Z, Y, X = shape
    N = Z * Y
    me = {a: lax.axis_index(a) for a in AXES}
    inv_centre, weights = sweep_weights()
    inv36 = 1.0 / 36.0
    half = SWEEPS
    last_q = 2 * half
    zero_slot = last_q + 2

    loads = [pltpu.make_async_copy(kap_hbm, c_ref, in_sem.at[0]),
             pltpu.make_async_copy(x0_hbm, v_ref.at[0, pl.ds(Y, N)], in_sem.at[1]),
             pltpu.make_async_copy(b_hbm, e_ref.at[0], in_sem.at[2])]
    for load in loads:
        load.start()

    for halo in (xhalo, yhalo, zhalo, zyhalo, zxhalo, yxhalo):
        halo[...] = jnp.zeros_like(halo)

    def offset(d):
        return {a: me[a] + s for a, s in zip(("gz", "gy", "gx"), d) if s}

    def has(d):
        cond = None
        for a, s in zip(("gz", "gy", "gx"), d):
            if s:
                one = me[a] > 0 if s < 0 else me[a] < sizes[a] - 1
                cond = one if cond is None else cond & one
        return cond

    DIRS = [d for d in DIRECTIONS
            if all(s == 0 or sizes[a] > 1 for a, s in zip(("gz", "gy", "gx"), d))]

    barrier = pltpu.get_barrier_semaphore()
    count = 0
    for d in DIRS:
        cond = has(d)

        def greet(d=d):
            pl.semaphore_signal(barrier, inc=1, device_id=offset(d), device_id_type=MESH)
        pl.when(cond)(greet)
        count = count + jnp.where(cond, 1, 0)
    for axes in phases:
        for peer in peers(sizes, me, axes):
            pl.semaphore_signal(barrier, inc=1, device_id=peer[0], device_id_type=MESH)
            count = count + 1

    guard = jnp.zeros((Y, X), jnp.float32)
    for j in range(last_q + 2):
        v_ref[j, 0:Y, :] = guard
        v_ref[j, Y + N:2 * Y + N, :] = guard
    u_ref[0:Y, :] = guard
    u_ref[Y + N:2 * Y + N, :] = guard
    for k in range(Z):
        e_ref[zero_slot, k * Y:(k + 1) * Y, :] = guard
        d_ref[k * Y:(k + 1) * Y, :] = guard

    lane = lax.broadcasted_iota(jnp.int32, (Y, X), 1)
    row = lax.broadcasted_iota(jnp.int32, (Y, X), 0)
    quarter, place = lane // 4, lane % 4
    left_half = place < 2
    first_x, last_x = lane == 0, lane == X - 1
    edge_x = first_x | last_x
    first_y, last_y = row == 0, row == Y - 1
    lane_z = lax.broadcasted_iota(jnp.int32, (Z, X), 1)
    row_z = lax.broadcasted_iota(jnp.int32, (Z, X), 0)

    at_lo, at_x, at_hi = Z, 2 * Z, 2 * Z + Y

    def pack_y(slot, src, off):
        for at, y in ((0, 1), (at_lo, 0), (at_hi, Y - 1), (at_hi + Z, Y - 2)):
            send[slot, at:at + Z, :] = src[pl.ds(off + y, Z, stride=Y), :]

    def pack_x(slot, src, off):
        acc = jnp.zeros((Y, X), jnp.float32)
        for k in range(Z):
            v = src[off + k * Y:off + (k + 1) * Y, :]
            acc = jnp.where(quarter == k, pltpu.roll(v, (2 + 4 * k) % X, 1), acc)
        send[slot, at_x:at_x + Y, :] = acc

    def source_of(d, slot, src, off):
        dz, dy, dx = d
        out = send.at[slot]
        if dx:
            if dy == 0:
                return out.at[pl.ds(at_x, Y)]
            return out.at[pl.ds(at_lo if dy < 0 else at_x, Z + Y)]
        if dy and dz:
            return out.at[pl.ds((at_lo if dy < 0 else at_hi) + (0 if dz < 0 else Z - 8), 8)]
        if dy:
            return out.at[pl.ds(0 if dy < 0 else at_hi, 2 * Z)]
        return src.at[pl.ds(off if dz < 0 else off + N - 2 * Y, 2 * Y)]

    def halo_of(d, slot):
        sz, sy, sx = (0 if s > 0 else 1 for s in d)
        dz, dy, dx = d
        if dx and dy:
            return yxhalo.at[slot, sy, sx]
        if dx and dz:
            return zxhalo.at[slot, sz, sx]
        if dx:
            return xhalo.at[slot, sx]
        if dy and dz:
            return zyhalo.at[slot, sz, sy]
        return yhalo.at[slot, sy] if dy else zhalo.at[slot, sz]

    def copy_to(d, slot, src, off):
        i = DIRECTIONS.index(d)
        return pltpu.make_async_remote_copy(
            src_ref=source_of(d, slot, src, off), dst_ref=halo_of(d, slot),
            send_sem=send_sem.at[slot, i], recv_sem=recv_sem.at[slot, i],
            device_id=offset(d), device_id_type=MESH)

    def copy_from(d, slot, src, off):
        back = tuple(-s for s in d)
        i = DIRECTIONS.index(back)
        return pltpu.make_async_remote_copy(
            src_ref=source_of(back, slot, src, off), dst_ref=halo_of(back, slot),
            send_sem=send_sem.at[slot, i], recv_sem=recv_sem.at[slot, i],
            device_id=offset(d), device_id_type=MESH)

    def start_all(slot, src, off):
        def go(want):
            for d in DIRS:
                if want(d):
                    pl.when(has(d))(lambda d=d: copy_to(d, slot, src, off).start())

        go(lambda d: d[1] == 0 and d[2] == 0)
        pack_x(slot, src, off)
        pack_y(slot, src, off)
        go(lambda d: d[2] != 0)
        go(lambda d: d[1] != 0 and d[2] == 0)

    def finish_all(slot, src, off):
        for d in DIRS:
            def done(d=d):
                copy_from(d, slot, src, off).wait_recv()
                copy_to(d, slot, src, off).wait_send()
            pl.when(has(d))(done)

    def faces(slot):
        z1 = [zhalo[slot, 0, Y:2 * Y, :], zhalo[slot, 1, 0:Y, :]]
        y1 = [yhalo[slot, 0, 0:Z, :], yhalo[slot, 1, Z:2 * Z, :]]
        x1 = jnp.where(left_half, xhalo[slot, 0], xhalo[slot, 1])
        return z1, y1, x1

    def pairs_of(columns):
        return jnp.where(place == 2, pltpu.roll(columns, 1, 1), pltpu.roll(columns, X - 1, 1))

    def edge_of(pairs, k):
        return jnp.where(edge_x, pltpu.roll(pairs, (2 * X - 2 - 4 * k) % X, 1), 0.0)

    def along_x(v, lanes):
        return (jnp.where(lanes == 0, 0.0, pltpu.roll(v, 1, 1))
                + jnp.where(lanes == X - 1, 0.0, pltpu.roll(v, X - 1, 1)))

    exists = {a: [jnp.where(me[a] > 0, 1.0, 0.0).astype(jnp.float32),
                  jnp.where(me[a] < sizes[a] - 1, 1.0, 0.0).astype(jnp.float32)] for a in AXES}

    def outer(slot, v, off):
        z1, y1, x1 = faces(slot)
        z2 = [zhalo[slot, 0, 0:Y, :], zhalo[slot, 1, Y:2 * Y, :]]
        y2 = [yhalo[slot, 0, Z:2 * Z, :], yhalo[slot, 1, 0:Z, :]]
        zx = [jnp.where(left_half, zxhalo[slot, s, 0], zxhalo[slot, s, 1]) for s in (0, 1)]
        yx = [jnp.where(left_half, yxhalo[slot, s, 0, r:r + Y, :], yxhalo[slot, s, 1, r:r + Y, :])
              for s, r in ((0, 0), (1, Z))]
        zy = [[zyhalo[slot, sz, sy, r:r + 1, :] for sy in (0, 1)] for sz, r in ((0, 7), (1, 0))]
        uz, uy = [], []
        for s, k in ((0, 0), (1, Z - 1)):
            f = z1[s]
            total = z2[s] + v[off + k * Y:off + (k + 1) * Y, :] + along_x(f, lane)
            total = total + edge_of(pairs_of(zx[s]), Z - 1 - k)
            total = total + jnp.where(first_y, zy[s][0], pltpu.roll(f, 1, 0))
            total = total + jnp.where(last_y, zy[s][1], pltpu.roll(f, Y - 1, 0))
            uz.append((cz_ref[s] * f - total) * exists["gz"][s])
        for s, at, r in ((0, at_lo, Y), (1, at_hi, 0)):
            f = y1[s]
            total = y2[s] + send[slot, at:at + Z, :]
            total = total + jnp.where(lane_z == 0, pltpu.roll(yxhalo[slot, s, 0, r:r + Z, :], 1, 1),
                                      pltpu.roll(f, 1, 1))
            total = total + jnp.where(lane_z == X - 1,
                                      pltpu.roll(yxhalo[slot, s, 1, r:r + Z, :], X - 1, 1),
                                      pltpu.roll(f, X - 1, 1))
            total = total + jnp.where(row_z == 0, zy[0][s], pltpu.roll(f, 1, 0))
            total = total + jnp.where(row_z == Z - 1, zy[1][s], pltpu.roll(f, Z - 1, 0))
            uy.append((cy_ref[s] * f - total) * exists["gy"][s])
        own = send[slot, at_x:at_x + Y, :]
        total = jnp.where(place == 1, pltpu.roll(x1, 1, 1) + pltpu.roll(own, X - 1, 1),
                          pltpu.roll(x1, X - 1, 1) + pltpu.roll(own, 1, 1))
        total = total + jnp.where(first_y, yx[0][Y - 1:Y, :], pltpu.roll(x1, 1, 0))
        total = total + jnp.where(last_y, yx[1][0:1, :], pltpu.roll(x1, Y - 1, 0))
        total = total + jnp.where(lane < 4, pltpu.roll(zx[0], 4, 1), pltpu.roll(x1, 4, 1))
        total = total + jnp.where(lane >= X - 4, pltpu.roll(zx[1], X - 4, 1),
                                  pltpu.roll(x1, X - 4, 1))
        ux = (cx_ref[...] * x1 - total) * jnp.where(left_half, exists["gx"][0], exists["gx"][1])
        return uz, uy, ux

    def k_inner(src, dst, dst_off):
        for k in range(Z):
            i = Y + k * Y
            v = src[i:i + Y, :]
            total = src[i - Y:i, :] + src[i + Y:i + 2 * Y, :] + along_x(v, lane)
            total = total + jnp.where(first_y, 0.0, src[i - 1:i - 1 + Y, :])
            total = total + jnp.where(last_y, 0.0, src[i + 1:i + 1 + Y, :])
            dst[dst_off + k * Y:dst_off + (k + 1) * Y, :] = c_ref[k * Y:(k + 1) * Y, :] * v - total

    def k_fix(dst, dst_off, halo, post):
        hz, hy, hx = halo
        for s, first in ((0, 0), (1, N - Y)):
            rows = slice(dst_off + first, dst_off + first + Y)
            dst[rows, :] = dst[rows, :] - hz[s]
        for s, first in ((0, 0), (1, Y - 1)):
            rows = pl.ds(dst_off + first, Z, stride=Y)
            dst[rows, :] = dst[rows, :] - hy[s]
        pairs = pairs_of(hx)
        for k in range(Z):
            rows = slice(dst_off + k * Y, dst_off + (k + 1) * Y)
            post(k, dst[rows, :] - edge_of(pairs, k))

    loads[0].wait()
    pl.semaphore_wait(barrier, count)
    start_all(2, c_ref, 0)
    loads[1].wait()
    start_all(0, v_ref.at[0], Y)
    loads[2].wait()
    finish_all(2, c_ref, 0)
    kz, ky, kx = faces(2)
    for s in (0, 1):
        cz_ref[s] = 6.0 + kz[s]
        cy_ref[s] = 6.0 + ky[s]
    cx_ref[...] = 6.0 + kx
    for k in range(Z):
        rows = slice(k * Y, (k + 1) * Y)
        c_ref[rows, :] = 6.0 + c_ref[rows, :]

    gathers = (gather_a, gather_b, gather_c)

    def red_start(i, value):
        part[i] = value
        gathers[i][pl.ds(rank(sizes, me, phases[i]), 1)] = value[None]
        for k, (peer, _) in enumerate(peers(sizes, me, phases[i])):
            pltpu.make_async_remote_copy(
                src_ref=part.at[i], dst_ref=gathers[i].at[rank(sizes, me, phases[i])],
                send_sem=red_send.at[i, k], recv_sem=red_recv.at[i, k],
                device_id=peer, device_id_type=MESH).start()

    def red_finish(i):
        for k, (peer, origin) in enumerate(peers(sizes, me, phases[i])):
            copy = pltpu.make_async_remote_copy(
                src_ref=part.at[i], dst_ref=gathers[i].at[rank(sizes, origin, phases[i])],
                send_sem=red_send.at[i, k], recv_sem=red_recv.at[i, k],
                device_id=peer, device_id_type=MESH)
            copy.wait_recv()
            copy.wait_send()
        total = gathers[i][0]
        for j in range(1, group_size(sizes, phases[i])):
            total = total + gathers[i][j]
        return total

    def red_first():
        rows8 = lax.broadcasted_iota(jnp.int32, (8, X), 0)
        mine = jnp.zeros((8, X), jnp.float32)
        for j, value in enumerate((sums_s[half - 1], sums_v[half], sums_s[last_q - 1], sums_u[...])):
            mine = jnp.where(rows8 == j, jnp.sum(value, axis=0, keepdims=True), mine)
        red_start(0, mine)

    def q_body(q, carry):
        phase = lax.rem(q, half)
        sweep = jnp.minimum(phase, 1)
        source = sweep * (1 + half * (q // half)) + (1 - sweep) * zero_slot * ((q + last_q - 1) // last_q)
        sign = jnp.where((sweep == 0) & (q > 0), -1.0, 1.0).astype(jnp.float32)
        old, new, keep = jnp.float32(0.0), sign * jnp.float32(inv_centre), jnp.float32(0.0)
        for j, (wo, wn) in enumerate(weights):
            old = jnp.where(phase == j + 1, jnp.float32(wo), old)
            new = jnp.where(phase == j + 1, jnp.float32(wn), new)
            keep = jnp.where(phase == j + 1, jnp.float32(1.0), keep)
        v = v_ref.at[q]
        v_new = v_ref.at[q + 1]
        zero8 = jnp.zeros((8, X), jnp.float32)
        acc = {"u": zero8, "s": zero8, "v": zero8}

        def fold(name, value):
            for j in range(0, Y, 8):
                acc[name] = acc[name] + value[j:j + 8]

        def post_u(k, value):
            u_ref[Y + k * Y:2 * Y + k * Y, :] = value
            fold("u", value * value)

        def post_t(k, t):
            rows = slice(k * Y, (k + 1) * Y)
            vrows = slice(Y + k * Y, 2 * Y + k * Y)
            t = t * inv36
            src = e_ref[source, rows, :]
            defect = src - t
            e_ref[q + 1, rows, :] = sign * defect
            upd = old * d_ref[rows, :] + new * defect
            d_ref[rows, :] = upd
            was = v[vrows, :]
            z = keep * was + upd
            v_new[vrows, :] = z
            fold("s", src * z)
            fold("v", was * t)

        slot = lax.rem(q, 2)
        pl.when(q > 0)(lambda: start_all(slot, v, Y))
        k_inner(v, u_ref, Y)
        finish_all(slot, v, Y)
        k_fix(u_ref, Y, faces(slot), post_u)
        sums_u[...] = acc["u"]
        pl.when(q == last_q)(red_first)
        k_inner(u_ref, t_ref, 0)
        k_fix(t_ref, 0, outer(slot, v, Y), post_t)
        sums_s[q] = acc["s"]
        sums_v[q] = acc["v"]
        return carry

    lax.fori_loop(0, last_q + 1, q_body, 0)

    total = red_finish(0)
    for i in range(1, len(phases)):
        red_start(i, total)
        total = red_finish(i)
    totals = jnp.sum(total, axis=1, keepdims=True)
    e0, g1, g2 = totals[0:1], totals[1:2], totals[2:3]
    g3 = totals[3:4] * inv36
    alpha = e0 / g1
    e1 = e0 - 2.0 * alpha * g1 + alpha * alpha * g2
    keep = 1.0 + e1 / e0
    den = keep * keep * g1 - 2.0 * keep * alpha * g2 + alpha * alpha * g3
    alpha1 = e1 / den
    p = alpha + alpha1 * keep
    q = alpha1 * alpha
    for k in range(Z):
        rows = slice(k * Y, (k + 1) * Y)
        vrows = slice(Y + k * Y, 2 * Y + k * Y)
        x_ref[rows, :] = v_ref[0, vrows, :] + p * v_ref[half, vrows, :] - q * v_ref[last_q, vrows, :]
        r_ref[rows, :] = e_ref[1, rows, :] - p * e_ref[half + 1, rows, :] + q * e_ref[last_q + 1, rows, :]


def body(sizes, right_side, initial, kappa_sq):
    Z, Y, X = right_side.shape
    N = Z * Y
    f32 = jnp.float32
    flat = lambda a: a.reshape(N, X)
    vm = pl.BlockSpec(memory_space=pltpu.VMEM)
    hbm = pl.BlockSpec(memory_space=pltpu.HBM)
    assert 4 * Z == X and Y % 8 == 0
    phases = [("gx", "gy"), ("gz",)] if sizes["gx"] * sizes["gy"] <= 16 else [(a,) for a in AXES]
    groups = [group_size(sizes, axes) for axes in phases] + [1]
    slots = 3
    count = 2 * SWEEPS + 1
    out = pl.pallas_call(
        functools.partial(kernel, sizes, phases, (Z, Y, X)),
        out_shape=[jax.ShapeDtypeStruct((N, X), f32)] * 2,
        in_specs=[hbm] * 3,
        out_specs=[vm] * 2,
        scratch_shapes=[
            pltpu.VMEM((count + 1, N + 2 * Y, X), f32),
            pltpu.VMEM((count + 2, N, X), f32),
            pltpu.VMEM((N + 2 * Y, X), f32),
            pltpu.VMEM((N, X), f32),
            pltpu.VMEM((N, X), f32),
            pltpu.VMEM((N, X), f32),
            pltpu.VMEM((slots, 4 * Z + Y, X), f32),
            pltpu.VMEM((slots, 2, Y, X), f32),
            pltpu.VMEM((slots, 2, 2 * Z, X), f32),
            pltpu.VMEM((slots, 2, 2 * Y, X), f32),
            pltpu.VMEM((slots, 2, 2, 8, X), f32),
            pltpu.VMEM((slots, 2, 2, Y, X), f32),
            pltpu.VMEM((slots, 2, 2, Z + Y, X), f32),
            pltpu.VMEM((2, Y, X), f32),
            pltpu.VMEM((2, Z, X), f32),
            pltpu.VMEM((Y, X), f32),
            pltpu.VMEM((count, 8, X), f32),
            pltpu.VMEM((count, 8, X), f32),
            pltpu.VMEM((8, X), f32),
            pltpu.VMEM((3, 8, X), f32),
        ] + [pltpu.VMEM(((groups + [1])[i], 8, X), f32) for i in range(3)] + [
            pltpu.SemaphoreType.DMA((slots, len(DIRECTIONS))),
            pltpu.SemaphoreType.DMA((slots, len(DIRECTIONS))),
            pltpu.SemaphoreType.DMA((3, max(groups))),
            pltpu.SemaphoreType.DMA((3, max(groups))),
            pltpu.SemaphoreType.DMA((3,)),
        ],
        compiler_params=pltpu.CompilerParams(
            collective_id=0, has_side_effects=True, vmem_limit_bytes=63 * 1024 * 1024),
        name="cg",
    )(flat(right_side), flat(initial), flat(kappa_sq))
    return tuple(o.reshape(Z, Y, X) for o in out)


def solution(mesh):
    spec = P("gz", "gy", "gx")
    sizes = {a: mesh.shape[a] for a in AXES}
    return jax.shard_map(functools.partial(body, sizes), mesh=mesh, in_specs=(spec,) * 3,
                         out_specs=(spec,) * 2, check_vma=False)
```

```python
import functools
import jax
import jax.numpy as jnp
from jax import lax
from jax.experimental import pallas as pl
from jax.experimental.pallas import tpu as pltpu
from jax.sharding import PartitionSpec as P

SWEEPS = 3
cheb_high = 7.2
cheb_low = 0.072
MESH = pl.DeviceIdType.MESH
AXES = ("gx", "gy", "gz")
DIRECTIONS = [(z, y, x) for z in (-1, 0, 1) for y in (-1, 0, 1) for x in (-1, 0, 1)
              if 1 <= abs(z) + abs(y) + abs(x) <= 2]


def group_size(sizes, axes):
    size = 1
    for a in axes:
        size *= sizes[a]
    return size


def rank(sizes, where, axes):
    index = 0
    for a in axes:
        index = index * sizes[a] + where[a]
    return index


def peers(sizes, me, axes):
    found = []
    for k in range(1, group_size(sizes, axes)):
        to, origin, left = {}, {}, k
        for a in reversed(axes):
            shift, left = left % sizes[a], left // sizes[a]
            to[a] = lax.rem(me[a] + shift, sizes[a])
            origin[a] = lax.rem(me[a] + sizes[a] - shift, sizes[a])
        found.append((to, origin))
    return found


def sweep_weights():
    centre = (cheb_high + cheb_low) / 2.0
    half_width = (cheb_high - cheb_low) / 2.0
    sigma = centre / half_width
    old = 1.0 / sigma
    weights = []
    for _ in range(SWEEPS - 1):
        new = 1.0 / (2.0 * sigma - old)
        weights.append((new * old, 2.0 * new / half_width))
        old = new
    return 1.0 / centre, weights


def kernel(sizes, phases, shape, b_hbm, x0_hbm, kap_hbm, x_ref, r_ref,
           v_ref, e_ref, u_ref, hrow, c_ref, d_ref,
           send, xhalo, yhalo, zhalo, zyhalo, zxhalo, yxhalo, cz_ref, cy_ref, cx_ref,
           sums_s, sums_v, sums_u, part, gather_a, gather_b, gather_c,
           send_sem, recv_sem, red_send, red_recv, in_sem):
    Z, Y, X = shape
    N = Z * Y
    me = {a: lax.axis_index(a) for a in AXES}
    inv_centre, weights = sweep_weights()
    inv36 = 1.0 / 36.0
    half = SWEEPS
    last_q = 2 * half
    zero_slot = last_q + 2

    loads = [pltpu.make_async_copy(kap_hbm, c_ref, in_sem.at[0]),
             pltpu.make_async_copy(x0_hbm, v_ref.at[0, pl.ds(Y, N)], in_sem.at[1]),
             pltpu.make_async_copy(b_hbm, e_ref.at[0], in_sem.at[2])]
    for load in loads:
        load.start()

    for halo in (xhalo, yhalo, zhalo, zyhalo, zxhalo, yxhalo):
        halo[...] = jnp.zeros_like(halo)

    other_x = sizes["gx"] == 2

    def offset(d):
        to = {a: me[a] + s for a, s in zip(("gz", "gy", "gx"), d) if s}
        if other_x and d[2]:
            to["gx"] = 1 - me["gx"]
        return to

    def has(d):
        cond = None
        for a, s in zip(("gz", "gy", "gx"), d):
            if s and not (other_x and a == "gx"):
                one = me[a] > 0 if s < 0 else me[a] < sizes[a] - 1
                cond = one if cond is None else cond & one
        return cond

    def when(cond, fn):
        if cond is None:
            fn()
        else:
            pl.when(cond)(fn)

    DIRS = [d for d in DIRECTIONS
            if all(s == 0 or sizes[a] > 1 for a, s in zip(("gz", "gy", "gx"), d))
            and not (other_x and d[2] < 0)]

    def reverse(d):
        return (-d[0], -d[1], d[2] if other_x else -d[2])

    barrier = pltpu.get_barrier_semaphore()
    count = 0
    for d in DIRS:
        cond = has(d)

        def greet(d=d):
            pl.semaphore_signal(barrier, inc=1, device_id=offset(d), device_id_type=MESH)
        when(cond, greet)
        count = count + (1 if cond is None else jnp.where(cond, 1, 0))
    for axes in phases:
        for peer in peers(sizes, me, axes):
            pl.semaphore_signal(barrier, inc=1, device_id=peer[0], device_id_type=MESH)
            count = count + 1

    guard = jnp.zeros((Y, X), jnp.float32)
    for j in range(last_q + 2):
        v_ref[j, 0:Y, :] = guard
        v_ref[j, Y + N:2 * Y + N, :] = guard
    u_ref[0:Y, :] = guard
    u_ref[Y + N:2 * Y + N, :] = guard
    for k in range(Z):
        e_ref[zero_slot, k * Y:(k + 1) * Y, :] = guard
        d_ref[k * Y:(k + 1) * Y, :] = guard

    lane = lax.broadcasted_iota(jnp.int32, (Y, X), 1)
    row = lax.broadcasted_iota(jnp.int32, (Y, X), 0)
    quarter, place = lane // 4, lane % 4
    left_half = place < 2
    first_x, last_x = lane == 0, lane == X - 1
    edge_x = first_x | last_x
    first_y, last_y = row == 0, row == Y - 1
    lane_z = lax.broadcasted_iota(jnp.int32, (Z, X), 1)
    row_z = lax.broadcasted_iota(jnp.int32, (Z, X), 0)

    at_lo, at_x, at_hi = Z, 2 * Z, 2 * Z + Y

    def pack_y(slot, src, off):
        for at, y in ((0, 1), (at_lo, 0), (at_hi, Y - 1), (at_hi + Z, Y - 2)):
            send[slot, at:at + Z, :] = src[pl.ds(off + y, Z, stride=Y), :]

    def pack_x(slot, src, off):
        acc = jnp.zeros((Y, X), jnp.float32)
        for k in range(Z):
            v = src[off + k * Y:off + (k + 1) * Y, :]
            acc = jnp.where(quarter == k, pltpu.roll(v, (2 + 4 * k) % X, 1), acc)
        send[slot, at_x:at_x + Y, :] = acc

    def source_of(d, slot, src, off):
        dz, dy, dx = d
        out = send.at[slot]
        if dx:
            if dy == 0:
                return out.at[pl.ds(at_x, Y)]
            return out.at[pl.ds(at_lo if dy < 0 else at_x, Z + Y)]
        if dy and dz:
            return out.at[pl.ds((at_lo if dy < 0 else at_hi) + (0 if dz < 0 else Z - 8), 8)]
        if dy:
            return out.at[pl.ds(0 if dy < 0 else at_hi, 2 * Z)]
        return src.at[pl.ds(off if dz < 0 else off + N - 2 * Y, 2 * Y)]

    def halo_of(d, slot, side_x):
        sz, sy = (0 if s > 0 else 1 for s in d[:2])
        sx = side_x if other_x else (0 if d[2] > 0 else 1)
        dz, dy, dx = d
        if dx and dy:
            return yxhalo.at[slot, sy, sx]
        if dx and dz:
            return zxhalo.at[slot, sz, sx]
        if dx:
            return xhalo.at[slot, sx]
        if dy and dz:
            return zyhalo.at[slot, sz, sy]
        return yhalo.at[slot, sy] if dy else zhalo.at[slot, sz]

    def copy_to(d, slot, src, off):
        i = DIRECTIONS.index(d)
        return pltpu.make_async_remote_copy(
            src_ref=source_of(d, slot, src, off), dst_ref=halo_of(d, slot, me["gx"]),
            send_sem=send_sem.at[slot, i], recv_sem=recv_sem.at[slot, i],
            device_id=offset(d), device_id_type=MESH)

    def copy_from(d, slot, src, off):
        back = reverse(d)
        i = DIRECTIONS.index(back)
        return pltpu.make_async_remote_copy(
            src_ref=source_of(back, slot, src, off), dst_ref=halo_of(back, slot, 1 - me["gx"]),
            send_sem=send_sem.at[slot, i], recv_sem=recv_sem.at[slot, i],
            device_id=offset(d), device_id_type=MESH)

    def start_all(slot, src, off, packed_x=False):
        def go(want):
            for d in DIRS:
                if want(d):
                    when(has(d), lambda d=d: copy_to(d, slot, src, off).start())

        if packed_x:
            go(lambda d: d[2] != 0 and d[1] == 0)
        pack_y(slot, src, off)
        if packed_x:
            go(lambda d: d[2] != 0 and d[1] != 0)
        go(lambda d: d[0] != 0 and d[1] != 0 and d[2] == 0)
        go(lambda d: d[1] != 0 and d[0] == 0 and d[2] == 0)
        go(lambda d: d[0] != 0 and d[1] == 0 and d[2] == 0)
        if not packed_x:
            pack_x(slot, src, off)
            go(lambda d: d[2] != 0)

    def finish(edges, slot, src, off):
        for d in DIRS:
            if (sum(1 for s in d if s) > 1) != edges:
                continue

            def done(d=d):
                copy_from(d, slot, src, off).wait_recv()
                copy_to(d, slot, src, off).wait_send()
            when(has(d), done)

    def faces(slot):
        z1 = [zhalo[slot, 0, Y:2 * Y, :], zhalo[slot, 1, 0:Y, :]]
        y1 = [yhalo[slot, 0, 0:Z, :], yhalo[slot, 1, Z:2 * Z, :]]
        x1 = jnp.where(left_half, xhalo[slot, 0], xhalo[slot, 1])
        return z1, y1, x1

    def pairs_of(columns):
        return jnp.where(place == 2, pltpu.roll(columns, 1, 1), pltpu.roll(columns, X - 1, 1))

    def edge_of(pairs, k):
        return jnp.where(edge_x, pltpu.roll(pairs, (2 * X - 2 - 4 * k) % X, 1), 0.0)

    def along_x(v, lanes):
        return (jnp.where(lanes == 0, 0.0, pltpu.roll(v, 1, 1))
                + jnp.where(lanes == X - 1, 0.0, pltpu.roll(v, X - 1, 1)))

    exists = {a: [jnp.where(me[a] > 0, 1.0, 0.0).astype(jnp.float32),
                  jnp.where(me[a] < sizes[a] - 1, 1.0, 0.0).astype(jnp.float32)] for a in AXES}

    def outer(slot, v, off):
        z1, y1, x1 = faces(slot)
        z2 = [zhalo[slot, 0, 0:Y, :], zhalo[slot, 1, Y:2 * Y, :]]
        y2 = [yhalo[slot, 0, Z:2 * Z, :], yhalo[slot, 1, 0:Z, :]]
        zx = [jnp.where(left_half, zxhalo[slot, s, 0], zxhalo[slot, s, 1]) for s in (0, 1)]
        yx = [jnp.where(left_half, yxhalo[slot, s, 0, r:r + Y, :], yxhalo[slot, s, 1, r:r + Y, :])
              for s, r in ((0, 0), (1, Z))]
        zy = [[zyhalo[slot, sz, sy, r:r + 1, :] for sy in (0, 1)] for sz, r in ((0, 7), (1, 0))]
        uz, uy = [], []
        for s, k in ((0, 0), (1, Z - 1)):
            f = z1[s]
            total = z2[s] + v[off + k * Y:off + (k + 1) * Y, :] + along_x(f, lane)
            total = total + edge_of(pairs_of(zx[s]), Z - 1 - k)
            total = total + jnp.where(first_y, zy[s][0], pltpu.roll(f, 1, 0))
            total = total + jnp.where(last_y, zy[s][1], pltpu.roll(f, Y - 1, 0))
            uz.append((cz_ref[s] * f - total) * exists["gz"][s])
        for s, at, r in ((0, at_lo, Y), (1, at_hi, 0)):
            f = y1[s]
            total = y2[s] + send[slot, at:at + Z, :]
            total = total + jnp.where(lane_z == 0, pltpu.roll(yxhalo[slot, s, 0, r:r + Z, :], 1, 1),
                                      pltpu.roll(f, 1, 1))
            total = total + jnp.where(lane_z == X - 1,
                                      pltpu.roll(yxhalo[slot, s, 1, r:r + Z, :], X - 1, 1),
                                      pltpu.roll(f, X - 1, 1))
            total = total + jnp.where(row_z == 0, zy[0][s], pltpu.roll(f, 1, 0))
            total = total + jnp.where(row_z == Z - 1, zy[1][s], pltpu.roll(f, Z - 1, 0))
            uy.append((cy_ref[s] * f - total) * exists["gy"][s])
        own = send[slot, at_x:at_x + Y, :]
        total = jnp.where(place == 1, pltpu.roll(x1, 1, 1) + pltpu.roll(own, X - 1, 1),
                          pltpu.roll(x1, X - 1, 1) + pltpu.roll(own, 1, 1))
        total = total + jnp.where(first_y, yx[0][Y - 1:Y, :], pltpu.roll(x1, 1, 0))
        total = total + jnp.where(last_y, yx[1][0:1, :], pltpu.roll(x1, Y - 1, 0))
        total = total + jnp.where(lane < 4, pltpu.roll(zx[0], 4, 1), pltpu.roll(x1, 4, 1))
        total = total + jnp.where(lane >= X - 4, pltpu.roll(zx[1], X - 4, 1),
                                  pltpu.roll(x1, X - 4, 1))
        ux = (cx_ref[...] * x1 - total) * jnp.where(left_half, exists["gx"][0], exists["gx"][1])
        return uz, uy, ux

    def k_inner(src, dst, dst_off):
        for k in range(Z):
            i = Y + k * Y
            v = src[i:i + Y, :]
            total = src[i - Y:i, :] + src[i + Y:i + 2 * Y, :] + along_x(v, lane)
            total = total + jnp.where(first_y, 0.0, src[i - 1:i - 1 + Y, :])
            total = total + jnp.where(last_y, 0.0, src[i + 1:i + 1 + Y, :])
            dst[dst_off + k * Y:dst_off + (k + 1) * Y, :] = c_ref[k * Y:(k + 1) * Y, :] * v - total

    def k_first(halo, post):
        hz, hy, hx = halo
        for s in (0, 1):
            hrow[s] = hy[s]
        pairs = pairs_of(hx)
        for k in range(Z):
            total = edge_of(pairs, k)
            total = total + jnp.where(first_y, hrow[0, k:k + 1, :], 0.0)
            total = total + jnp.where(last_y, hrow[1, k:k + 1, :], 0.0)
            if k == 0:
                total = total + hz[0]
            if k == Z - 1:
                total = total + hz[1]
            post(k, u_ref[Y + k * Y:2 * Y + k * Y, :] - total)

    def k_second(halo, post):
        hz, hy, hx = halo
        u_ref[0:Y, :] = hz[0]
        u_ref[Y + N:2 * Y + N, :] = hz[1]
        for s in (0, 1):
            hrow[s] = hy[s]
        pairs = pairs_of(hx)
        for k in range(Z):
            i = Y + k * Y
            f = u_ref[i:i + Y, :]
            ends = pltpu.roll(pairs, (2 * X - 2 - 4 * k) % X, 1)
            total = u_ref[i - Y:i, :] + u_ref[i + Y:i + 2 * Y, :]
            total = total + jnp.where(first_x, ends, pltpu.roll(f, 1, 1))
            total = total + jnp.where(last_x, ends, pltpu.roll(f, X - 1, 1))
            total = total + jnp.where(first_y, hrow[0, k:k + 1, :], u_ref[i - 1:i - 1 + Y, :])
            total = total + jnp.where(last_y, hrow[1, k:k + 1, :], u_ref[i + 1:i + 1 + Y, :])
            post(k, c_ref[k * Y:(k + 1) * Y, :] * f - total)

    loads[0].wait()
    pl.semaphore_wait(barrier, count)
    start_all(2, c_ref, 0)
    loads[1].wait()
    start_all(0, v_ref.at[0], Y)
    loads[2].wait()
    finish(False, 2, c_ref, 0)
    finish(True, 2, c_ref, 0)
    kz, ky, kx = faces(2)
    for s in (0, 1):
        cz_ref[s] = 6.0 + kz[s]
        cy_ref[s] = 6.0 + ky[s]
    cx_ref[...] = 6.0 + kx
    for k in range(Z):
        rows = slice(k * Y, (k + 1) * Y)
        c_ref[rows, :] = 6.0 + c_ref[rows, :]

    gathers = (gather_a, gather_b, gather_c)

    def red_start(i, value):
        part[i] = value
        gathers[i][pl.ds(rank(sizes, me, phases[i]), 1)] = value[None]
        for k, (peer, _) in enumerate(peers(sizes, me, phases[i])):
            pltpu.make_async_remote_copy(
                src_ref=part.at[i], dst_ref=gathers[i].at[rank(sizes, me, phases[i])],
                send_sem=red_send.at[i, k], recv_sem=red_recv.at[i, k],
                device_id=peer, device_id_type=MESH).start()

    def red_finish(i):
        for k, (peer, origin) in enumerate(peers(sizes, me, phases[i])):
            copy = pltpu.make_async_remote_copy(
                src_ref=part.at[i], dst_ref=gathers[i].at[rank(sizes, origin, phases[i])],
                send_sem=red_send.at[i, k], recv_sem=red_recv.at[i, k],
                device_id=peer, device_id_type=MESH)
            copy.wait_recv()
            copy.wait_send()
        total = gathers[i][0]
        for j in range(1, group_size(sizes, phases[i])):
            total = total + gathers[i][j]
        return total

    def red_first():
        rows8 = lax.broadcasted_iota(jnp.int32, (8, X), 0)
        mine = jnp.zeros((8, X), jnp.float32)
        for j, value in enumerate((sums_s[half - 1], sums_v[half], sums_s[last_q - 1], sums_u[...])):
            mine = jnp.where(rows8 == j, jnp.sum(value, axis=0, keepdims=True), mine)
        red_start(0, mine)

    def q_body(q, carry):
        phase = lax.rem(q, half)
        sweep = jnp.minimum(phase, 1)
        source = sweep * (1 + half * (q // half)) + (1 - sweep) * zero_slot * ((q + last_q - 1) // last_q)
        sign = jnp.where((sweep == 0) & (q > 0), -1.0, 1.0).astype(jnp.float32)
        old, new, keep = jnp.float32(0.0), sign * jnp.float32(inv_centre), jnp.float32(0.0)
        for j, (wo, wn) in enumerate(weights):
            old = jnp.where(phase == j + 1, jnp.float32(wo), old)
            new = jnp.where(phase == j + 1, jnp.float32(wn), new)
            keep = jnp.where(phase == j + 1, jnp.float32(1.0), keep)
        v = v_ref.at[q]
        v_new = v_ref.at[q + 1]
        zero8 = jnp.zeros((8, X), jnp.float32)
        acc = {"u": zero8, "s": zero8, "v": zero8, "x": jnp.zeros((Y, X), jnp.float32)}

        def fold(name, value):
            for j in range(0, Y, 8):
                acc[name] = acc[name] + value[j:j + 8]

        def post_u(k, value):
            u_ref[Y + k * Y:2 * Y + k * Y, :] = value
            fold("u", value * value)

        def post_t(k, t):
            rows = slice(k * Y, (k + 1) * Y)
            vrows = slice(Y + k * Y, 2 * Y + k * Y)
            t = t * inv36
            src = e_ref[source, rows, :]
            defect = src - t
            e_ref[q + 1, rows, :] = sign * defect
            upd = old * d_ref[rows, :] + new * defect
            d_ref[rows, :] = upd
            was = v[vrows, :]
            z = keep * was + upd
            v_new[vrows, :] = z
            fold("s", src * z)
            fold("v", was * t)
            acc["x"] = jnp.where(quarter == k, pltpu.roll(z, (2 + 4 * k) % X, 1), acc["x"])

        slot = lax.rem(q, 2)
        k_inner(v, u_ref, Y)
        finish(False, slot, v, Y)
        k_first(faces(slot), post_u)
        sums_u[...] = acc["u"]
        pl.when(q == last_q)(red_first)
        finish(True, slot, v, Y)
        k_second(outer(slot, v, Y), post_t)
        send[1 - slot, at_x:at_x + Y, :] = acc["x"]
        pl.when(q < last_q)(lambda: start_all(1 - slot, v_new, Y, packed_x=True))
        sums_s[q] = acc["s"]
        sums_v[q] = acc["v"]
        return carry

    lax.fori_loop(0, last_q + 1, q_body, 0)

    total = red_finish(0)
    for i in range(1, len(phases)):
        red_start(i, total)
        total = red_finish(i)
    totals = jnp.sum(total, axis=1, keepdims=True)
    e0, g1, g2 = totals[0:1], totals[1:2], totals[2:3]
    g3 = totals[3:4] * inv36
    alpha = e0 / g1
    e1 = e0 - 2.0 * alpha * g1 + alpha * alpha * g2
    keep = 1.0 + e1 / e0
    den = keep * keep * g1 - 2.0 * keep * alpha * g2 + alpha * alpha * g3
    alpha1 = e1 / den
    p = alpha + alpha1 * keep
    q = alpha1 * alpha
    for k in range(Z):
        rows = slice(k * Y, (k + 1) * Y)
        vrows = slice(Y + k * Y, 2 * Y + k * Y)
        x_ref[rows, :] = v_ref[0, vrows, :] + p * v_ref[half, vrows, :] - q * v_ref[last_q, vrows, :]
        r_ref[rows, :] = e_ref[1, rows, :] - p * e_ref[half + 1, rows, :] + q * e_ref[last_q + 1, rows, :]


PIECES = 4


def hand_on(x_in, r_in, x_out, r_out, sem):
    copies = []
    for i, (src, dst) in enumerate(((x_in, x_out), (r_in, r_out))):
        n = src.shape[0] // PIECES
        for j in range(PIECES):
            rows = pl.ds(j * n, n)
            copies.append(pltpu.make_async_copy(src.at[rows], dst.at[rows], sem.at[i, j]))
    for copy in copies:
        copy.start()
    for copy in copies:
        copy.wait()


def body(sizes, right_side, initial, kappa_sq):
    Z, Y, X = right_side.shape
    N = Z * Y
    f32 = jnp.float32
    flat = lambda a: a.reshape(N, X)
    vm = pl.BlockSpec(memory_space=pltpu.VMEM)
    hbm = pl.BlockSpec(memory_space=pltpu.HBM)
    assert 4 * Z == X and Y % 8 == 0
    phases = [("gx", "gy"), ("gz",)] if sizes["gx"] * sizes["gy"] <= 16 else [(a,) for a in AXES]
    groups = [group_size(sizes, axes) for axes in phases] + [1]
    slots = 3
    count = 2 * SWEEPS + 1
    out = pl.pallas_call(
        functools.partial(kernel, sizes, phases, (Z, Y, X)),
        out_shape=[jax.ShapeDtypeStruct((N, X), f32)] * 2,
        in_specs=[hbm] * 3,
        out_specs=[vm] * 2,
        scratch_shapes=[
            pltpu.VMEM((count + 1, N + 2 * Y, X), f32),
            pltpu.VMEM((count + 2, N, X), f32),
            pltpu.VMEM((N + 2 * Y, X), f32),
            pltpu.VMEM((2, Z, X), f32),
            pltpu.VMEM((N, X), f32),
            pltpu.VMEM((N, X), f32),
            pltpu.VMEM((slots, 4 * Z + Y, X), f32),
            pltpu.VMEM((slots, 2, Y, X), f32),
            pltpu.VMEM((slots, 2, 2 * Z, X), f32),
            pltpu.VMEM((slots, 2, 2 * Y, X), f32),
            pltpu.VMEM((slots, 2, 2, 8, X), f32),
            pltpu.VMEM((slots, 2, 2, Y, X), f32),
            pltpu.VMEM((slots, 2, 2, Z + Y, X), f32),
            pltpu.VMEM((2, Y, X), f32),
            pltpu.VMEM((2, Z, X), f32),
            pltpu.VMEM((Y, X), f32),
            pltpu.VMEM((count, 8, X), f32),
            pltpu.VMEM((count, 8, X), f32),
            pltpu.VMEM((8, X), f32),
            pltpu.VMEM((3, 8, X), f32),
        ] + [pltpu.VMEM(((groups + [1])[i], 8, X), f32) for i in range(3)] + [
            pltpu.SemaphoreType.DMA((slots, len(DIRECTIONS))),
            pltpu.SemaphoreType.DMA((slots, len(DIRECTIONS))),
            pltpu.SemaphoreType.DMA((3, max(groups))),
            pltpu.SemaphoreType.DMA((3, max(groups))),
            pltpu.SemaphoreType.DMA((3,)),
        ],
        compiler_params=pltpu.CompilerParams(
            collective_id=0, has_side_effects=True, vmem_limit_bytes=63 * 1024 * 1024),
        name="cg",
    )(flat(right_side), flat(initial), flat(kappa_sq))
    out = pl.pallas_call(
        hand_on,
        out_shape=[jax.ShapeDtypeStruct((N, X), f32)] * 2,
        in_specs=[hbm] * 2,
        out_specs=[hbm] * 2,
        scratch_shapes=[pltpu.SemaphoreType.DMA((2, PIECES))],
        compiler_params=pltpu.CompilerParams(vmem_limit_bytes=63 * 1024 * 1024),
        name="hand_on",
    )(*out)
    return tuple(o.reshape(Z, Y, X) for o in out)


def solution(mesh):
    spec = P("gz", "gy", "gx")
    sizes = {a: mesh.shape[a] for a in AXES}
    return jax.shard_map(functools.partial(body, sizes), mesh=mesh, in_specs=(spec,) * 3,
                         out_specs=(spec,) * 2, check_vma=False)
```

```python
import functools
import jax
import jax.numpy as jnp
from jax import lax
from jax.experimental import pallas as pl
from jax.experimental.pallas import tpu as pltpu
from jax.sharding import PartitionSpec as P

SWEEPS = 3
cheb_high = 7.2
cheb_low = 0.072
MESH = pl.DeviceIdType.MESH
AXES = ("gx", "gy", "gz")
DIRECTIONS = [(z, y, x) for z in (-1, 0, 1) for y in (-1, 0, 1) for x in (-1, 0, 1)
              if 1 <= abs(z) + abs(y) + abs(x) <= 2]


def group_size(sizes, axes):
    size = 1
    for a in axes:
        size *= sizes[a]
    return size


def rank(sizes, where, axes):
    index = 0
    for a in axes:
        index = index * sizes[a] + where[a]
    return index


def peers(sizes, me, axes):
    found = []
    for k in range(1, group_size(sizes, axes)):
        to, origin, left = {}, {}, k
        for a in reversed(axes):
            shift, left = left % sizes[a], left // sizes[a]
            to[a] = lax.rem(me[a] + shift, sizes[a])
            origin[a] = lax.rem(me[a] + sizes[a] - shift, sizes[a])
        found.append((to, origin))
    return found


def sweep_weights():
    centre = (cheb_high + cheb_low) / 2.0
    half_width = (cheb_high - cheb_low) / 2.0
    sigma = centre / half_width
    old = 1.0 / sigma
    weights = []
    for _ in range(SWEEPS - 1):
        new = 1.0 / (2.0 * sigma - old)
        weights.append((new * old, 2.0 * new / half_width))
        old = new
    return 1.0 / centre, weights


def kernel(sizes, phases, shape, b_hbm, x0_hbm, kap_hbm, x_ref, r_ref,
           v, src_ref, v_hist, s_hist, u_ref, hrow, c_ref, d_ref,
           send, xhalo, yhalo, zhalo, zyhalo, zxhalo, yxhalo, cz_ref, cy_ref, cx_ref,
           sums_s, sums_v, sums_u, part, gather_a, gather_b, gather_c,
           send_sem, recv_sem, red_send, red_recv, in_sem):
    Z, Y, X = shape
    N = Z * Y
    me = {a: lax.axis_index(a) for a in AXES}
    inv_centre, weights = sweep_weights()
    inv36 = 1.0 / 36.0
    half = SWEEPS
    last_q = 2 * half

    loads = [pltpu.make_async_copy(kap_hbm, c_ref, in_sem.at[0]),
             pltpu.make_async_copy(x0_hbm, v.at[pl.ds(Y, N)], in_sem.at[1]),
             pltpu.make_async_copy(b_hbm, src_ref, in_sem.at[2])]
    for load in loads:
        load.start()

    for halo in (xhalo, yhalo, zhalo, zyhalo, zxhalo, yxhalo):
        halo[...] = jnp.zeros_like(halo)

    other_x = sizes["gx"] == 2

    def offset(d):
        to = {a: me[a] + s for a, s in zip(("gz", "gy", "gx"), d) if s}
        if other_x and d[2]:
            to["gx"] = 1 - me["gx"]
        return to

    def has(d):
        cond = None
        for a, s in zip(("gz", "gy", "gx"), d):
            if s and not (other_x and a == "gx"):
                one = me[a] > 0 if s < 0 else me[a] < sizes[a] - 1
                cond = one if cond is None else cond & one
        return cond

    def when(cond, fn):
        if cond is None:
            fn()
        else:
            pl.when(cond)(fn)

    DIRS = [d for d in DIRECTIONS
            if all(s == 0 or sizes[a] > 1 for a, s in zip(("gz", "gy", "gx"), d))
            and not (other_x and d[2] < 0)]

    def reverse(d):
        return (-d[0], -d[1], d[2] if other_x else -d[2])

    barrier = pltpu.get_barrier_semaphore()
    count = 0
    for d in DIRS:
        cond = has(d)

        def greet(d=d):
            pl.semaphore_signal(barrier, inc=1, device_id=offset(d), device_id_type=MESH)
        when(cond, greet)
        count = count + (1 if cond is None else jnp.where(cond, 1, 0))
    for axes in phases:
        for peer in peers(sizes, me, axes):
            pl.semaphore_signal(barrier, inc=1, device_id=peer[0], device_id_type=MESH)
            count = count + 1

    guard = jnp.zeros((Y, X), jnp.float32)
    for ref in (v, u_ref):
        ref[0:Y, :] = guard
        ref[Y + N:2 * Y + N, :] = guard
    for k in range(Z):
        d_ref[k * Y:(k + 1) * Y, :] = guard

    lane = lax.broadcasted_iota(jnp.int32, (Y, X), 1)
    row = lax.broadcasted_iota(jnp.int32, (Y, X), 0)
    quarter, place = lane // 4, lane % 4
    left_half = place < 2
    first_x, last_x = lane == 0, lane == X - 1
    edge_x = first_x | last_x
    first_y, last_y = row == 0, row == Y - 1
    lane_z = lax.broadcasted_iota(jnp.int32, (Z, X), 1)
    row_z = lax.broadcasted_iota(jnp.int32, (Z, X), 0)

    at_lo, at_x, at_hi = Z, 2 * Z, 2 * Z + Y

    def pack_y(slot, src, off):
        for at, y in ((0, 1), (at_lo, 0), (at_hi, Y - 1), (at_hi + Z, Y - 2)):
            send[slot, at:at + Z, :] = src[pl.ds(off + y, Z, stride=Y), :]

    def pack_x(slot, src, off):
        acc = jnp.zeros((Y, X), jnp.float32)
        for k in range(Z):
            v = src[off + k * Y:off + (k + 1) * Y, :]
            acc = jnp.where(quarter == k, pltpu.roll(v, (2 + 4 * k) % X, 1), acc)
        send[slot, at_x:at_x + Y, :] = acc

    def source_of(d, slot, src, off):
        dz, dy, dx = d
        out = send.at[slot]
        if dx:
            if dy == 0:
                return out.at[pl.ds(at_x, Y)]
            return out.at[pl.ds(at_x if dy < 0 else at_x + Y - 8, 8)]
        if dy and dz:
            return out.at[pl.ds((at_lo if dy < 0 else at_hi) + (0 if dz < 0 else Z - 8), 8)]
        if dy:
            return out.at[pl.ds(0 if dy < 0 else at_hi, 2 * Z)]
        return src.at[pl.ds(off if dz < 0 else off + N - 2 * Y, 2 * Y)]

    def halo_of(d, slot, side_x):
        sz, sy = (0 if s > 0 else 1 for s in d[:2])
        sx = side_x if other_x else (0 if d[2] > 0 else 1)
        dz, dy, dx = d
        if dx and dy:
            return yxhalo.at[slot, sy, sx]
        if dx and dz:
            return zxhalo.at[slot, sz, sx]
        if dx:
            return xhalo.at[slot, sx]
        if dy and dz:
            return zyhalo.at[slot, sz, sy]
        return yhalo.at[slot, sy] if dy else zhalo.at[slot, sz]

    def copy_to(d, slot, src, off):
        i = DIRECTIONS.index(d)
        return pltpu.make_async_remote_copy(
            src_ref=source_of(d, slot, src, off), dst_ref=halo_of(d, slot, me["gx"]),
            send_sem=send_sem.at[slot, i], recv_sem=recv_sem.at[slot, i],
            device_id=offset(d), device_id_type=MESH)

    def copy_from(d, slot, src, off):
        back = reverse(d)
        i = DIRECTIONS.index(back)
        return pltpu.make_async_remote_copy(
            src_ref=source_of(back, slot, src, off), dst_ref=halo_of(back, slot, 1 - me["gx"]),
            send_sem=send_sem.at[slot, i], recv_sem=recv_sem.at[slot, i],
            device_id=offset(d), device_id_type=MESH)

    def start_all(slot, src, off, packed_x=False):
        def go(want):
            for d in DIRS:
                if want(d):
                    when(has(d), lambda d=d: copy_to(d, slot, src, off).start())

        if packed_x:
            go(lambda d: d[2] != 0 and d[1] == 0)
        pack_y(slot, src, off)
        if packed_x:
            go(lambda d: d[2] != 0 and d[1] != 0)
        go(lambda d: d[0] != 0 and d[1] != 0 and d[2] == 0)
        go(lambda d: d[1] != 0 and d[0] == 0 and d[2] == 0)
        go(lambda d: d[0] != 0 and d[1] == 0 and d[2] == 0)
        if not packed_x:
            pack_x(slot, src, off)
            go(lambda d: d[2] != 0)

    def finish(edges, slot, src, off):
        for d in DIRS:
            if (sum(1 for s in d if s) > 1) != edges:
                continue

            def done(d=d):
                copy_from(d, slot, src, off).wait_recv()
                copy_to(d, slot, src, off).wait_send()
            when(has(d), done)

    def faces(slot):
        z1 = [zhalo[slot, 0, Y:2 * Y, :], zhalo[slot, 1, 0:Y, :]]
        y1 = [yhalo[slot, 0, 0:Z, :], yhalo[slot, 1, Z:2 * Z, :]]
        x1 = jnp.where(left_half, xhalo[slot, 0], xhalo[slot, 1])
        return z1, y1, x1

    def pairs_of(columns):
        return jnp.where(place == 2, pltpu.roll(columns, 1, 1), pltpu.roll(columns, X - 1, 1))

    def edge_of(pairs, k):
        return jnp.where(edge_x, pltpu.roll(pairs, (2 * X - 2 - 4 * k) % X, 1), 0.0)

    def along_x(v, lanes):
        return (jnp.where(lanes == 0, 0.0, pltpu.roll(v, 1, 1))
                + jnp.where(lanes == X - 1, 0.0, pltpu.roll(v, X - 1, 1)))

    exists = {a: [jnp.where(me[a] > 0, 1.0, 0.0).astype(jnp.float32),
                  jnp.where(me[a] < sizes[a] - 1, 1.0, 0.0).astype(jnp.float32)] for a in AXES}

    def outer(slot, v, off):
        z1, y1, x1 = faces(slot)
        z2 = [zhalo[slot, 0, 0:Y, :], zhalo[slot, 1, Y:2 * Y, :]]
        y2 = [yhalo[slot, 0, Z:2 * Z, :], yhalo[slot, 1, 0:Z, :]]
        zx = [jnp.where(left_half, zxhalo[slot, s, 0], zxhalo[slot, s, 1]) for s in (0, 1)]
        yx = [jnp.where(left_half[0:1], yxhalo[slot, s, 0, r:r + 1, :], yxhalo[slot, s, 1, r:r + 1, :])
              for s, r in ((0, 7), (1, 0))]
        zy = [[zyhalo[slot, sz, sy, r:r + 1, :] for sy in (0, 1)] for sz, r in ((0, 7), (1, 0))]
        uz, uy = [], []
        for s, k in ((0, 0), (1, Z - 1)):
            f = z1[s]
            total = z2[s] + v[off + k * Y:off + (k + 1) * Y, :] + along_x(f, lane)
            total = total + edge_of(pairs_of(zx[s]), Z - 1 - k)
            total = total + jnp.where(first_y, zy[s][0], pltpu.roll(f, 1, 0))
            total = total + jnp.where(last_y, zy[s][1], pltpu.roll(f, Y - 1, 0))
            uz.append((cz_ref[s] * f - total) * exists["gz"][s])
        for s, at in ((0, at_lo), (1, at_hi)):
            f = y1[s]
            total = y2[s] + send[slot, at:at + Z, :]
            low, high = (jnp.sum(jnp.where(lane_z == 4 * row_z + j, yx[s], 0.0), axis=1, keepdims=True)
                         for j in (1, 2))
            total = total + jnp.where(lane_z == 0, low, pltpu.roll(f, 1, 1))
            total = total + jnp.where(lane_z == X - 1, high, pltpu.roll(f, X - 1, 1))
            total = total + jnp.where(row_z == 0, zy[0][s], pltpu.roll(f, 1, 0))
            total = total + jnp.where(row_z == Z - 1, zy[1][s], pltpu.roll(f, Z - 1, 0))
            uy.append((cy_ref[s] * f - total) * exists["gy"][s])
        own = send[slot, at_x:at_x + Y, :]
        total = jnp.where(place == 1, pltpu.roll(x1, 1, 1) + pltpu.roll(own, X - 1, 1),
                          pltpu.roll(x1, X - 1, 1) + pltpu.roll(own, 1, 1))
        total = total + jnp.where(first_y, yx[0], pltpu.roll(x1, 1, 0))
        total = total + jnp.where(last_y, yx[1], pltpu.roll(x1, Y - 1, 0))
        total = total + jnp.where(lane < 4, pltpu.roll(zx[0], 4, 1), pltpu.roll(x1, 4, 1))
        total = total + jnp.where(lane >= X - 4, pltpu.roll(zx[1], X - 4, 1),
                                  pltpu.roll(x1, X - 4, 1))
        ux = (cx_ref[...] * x1 - total) * jnp.where(left_half, exists["gx"][0], exists["gx"][1])
        return uz, uy, ux

    def k_inner(src, dst, dst_off):
        for k in range(Z):
            i = Y + k * Y
            v = src[i:i + Y, :]
            total = src[i - Y:i, :] + src[i + Y:i + 2 * Y, :] + along_x(v, lane)
            total = total + jnp.where(first_y, 0.0, src[i - 1:i - 1 + Y, :])
            total = total + jnp.where(last_y, 0.0, src[i + 1:i + 1 + Y, :])
            dst[dst_off + k * Y:dst_off + (k + 1) * Y, :] = c_ref[k * Y:(k + 1) * Y, :] * v - total

    def k_first(halo, post):
        hz, hy, hx = halo
        for s in (0, 1):
            hrow[s] = hy[s]
        pairs = pairs_of(hx)
        for k in range(Z):
            total = edge_of(pairs, k)
            total = total + jnp.where(first_y, hrow[0, k:k + 1, :], 0.0)
            total = total + jnp.where(last_y, hrow[1, k:k + 1, :], 0.0)
            if k == 0:
                total = total + hz[0]
            if k == Z - 1:
                total = total + hz[1]
            post(k, u_ref[Y + k * Y:2 * Y + k * Y, :] - total)

    def k_second(halo, post):
        hz, hy, hx = halo
        u_ref[0:Y, :] = hz[0]
        u_ref[Y + N:2 * Y + N, :] = hz[1]
        for s in (0, 1):
            hrow[s] = hy[s]
        pairs = pairs_of(hx)
        for k in range(Z):
            i = Y + k * Y
            f = u_ref[i:i + Y, :]
            ends = pltpu.roll(pairs, (2 * X - 2 - 4 * k) % X, 1)
            total = u_ref[i - Y:i, :] + u_ref[i + Y:i + 2 * Y, :]
            total = total + jnp.where(first_x, ends, pltpu.roll(f, 1, 1))
            total = total + jnp.where(last_x, ends, pltpu.roll(f, X - 1, 1))
            total = total + jnp.where(first_y, hrow[0, k:k + 1, :], u_ref[i - 1:i - 1 + Y, :])
            total = total + jnp.where(last_y, hrow[1, k:k + 1, :], u_ref[i + 1:i + 1 + Y, :])
            post(k, c_ref[k * Y:(k + 1) * Y, :] * f - total)

    loads[0].wait()
    pl.semaphore_wait(barrier, count)
    start_all(2, c_ref, 0)
    loads[1].wait()
    start_all(0, v, Y)
    for k in range(Z):
        v_hist[0, k * Y:(k + 1) * Y, :] = v[Y + k * Y:2 * Y + k * Y, :]
    loads[2].wait()
    finish(False, 2, c_ref, 0)
    finish(True, 2, c_ref, 0)
    kz, ky, kx = faces(2)
    for s in (0, 1):
        cz_ref[s] = 6.0 + kz[s]
        cy_ref[s] = 6.0 + ky[s]
    cx_ref[...] = 6.0 + kx
    for k in range(Z):
        rows = slice(k * Y, (k + 1) * Y)
        c_ref[rows, :] = 6.0 + c_ref[rows, :]

    gathers = (gather_a, gather_b, gather_c)

    def red_start(i, value):
        part[i] = value
        gathers[i][pl.ds(rank(sizes, me, phases[i]), 1)] = value[None]
        for k, (peer, _) in enumerate(peers(sizes, me, phases[i])):
            pltpu.make_async_remote_copy(
                src_ref=part.at[i], dst_ref=gathers[i].at[rank(sizes, me, phases[i])],
                send_sem=red_send.at[i, k], recv_sem=red_recv.at[i, k],
                device_id=peer, device_id_type=MESH).start()

    def red_finish(i):
        for k, (peer, origin) in enumerate(peers(sizes, me, phases[i])):
            copy = pltpu.make_async_remote_copy(
                src_ref=part.at[i], dst_ref=gathers[i].at[rank(sizes, origin, phases[i])],
                send_sem=red_send.at[i, k], recv_sem=red_recv.at[i, k],
                device_id=peer, device_id_type=MESH)
            copy.wait_recv()
            copy.wait_send()
        total = gathers[i][0]
        for j in range(1, group_size(sizes, phases[i])):
            total = total + gathers[i][j]
        return total

    def red_first():
        rows8 = lax.broadcasted_iota(jnp.int32, (8, X), 0)
        mine = jnp.zeros((8, X), jnp.float32)
        for j, value in enumerate((sums_s[half - 1], sums_v[half], sums_s[last_q - 1], sums_u[...])):
            mine = jnp.where(rows8 == j, jnp.sum(value, axis=0, keepdims=True), mine)
        red_start(0, mine)

    def q_body(q, carry):
        phase = lax.rem(q, half)
        sweep = jnp.minimum(phase, 1)
        sweeping = (sweep > 0).astype(jnp.float32)
        sign = jnp.where(q > 0, -1.0, 1.0).astype(jnp.float32)
        use_src = jnp.where((sweep > 0) | (q == 0), 1.0, 0.0).astype(jnp.float32)
        take = (1.0 - sweeping) * sign
        old, new = jnp.float32(0.0), sign * jnp.float32(inv_centre)
        for j, (wo, wn) in enumerate(weights):
            old = jnp.where(phase == j + 1, jnp.float32(wo), old)
            new = jnp.where(phase == j + 1, jnp.float32(wn), new)
        zero8 = jnp.zeros((8, X), jnp.float32)
        acc = {"u": zero8, "s": zero8, "v": zero8, "x": jnp.zeros((Y, X), jnp.float32)}

        def fold(name, value):
            for j in range(0, Y, 8):
                acc[name] = acc[name] + value[j:j + 8]

        def post_u(k, value):
            u_ref[Y + k * Y:2 * Y + k * Y, :] = value
            fold("u", value * value)

        def post_t(k, t):
            rows = slice(k * Y, (k + 1) * Y)
            vrows = slice(Y + k * Y, 2 * Y + k * Y)
            t = t * inv36
            src = src_ref[rows, :]
            defect = use_src * src - t
            kept = sweeping * src + take * defect
            src_ref[rows, :] = kept
            s_hist[q, rows, :] = kept
            upd = old * d_ref[rows, :] + new * defect
            d_ref[rows, :] = upd
            was = v[vrows, :]
            z = sweeping * was + upd
            v[vrows, :] = z
            v_hist[q + 1, rows, :] = z
            fold("s", src * z)
            fold("v", was * t)
            acc["x"] = jnp.where(quarter == k, pltpu.roll(z, (2 + 4 * k) % X, 1), acc["x"])

        slot = lax.rem(q, 2)
        k_inner(v, u_ref, Y)
        finish(False, slot, v, Y)
        k_first(faces(slot), post_u)
        sums_u[...] = acc["u"]
        pl.when(q == last_q)(red_first)
        finish(True, slot, v, Y)
        k_second(outer(slot, v, Y), post_t)
        send[1 - slot, at_x:at_x + Y, :] = acc["x"]
        pl.when(q < last_q)(lambda: start_all(1 - slot, v, Y, packed_x=True))
        sums_s[q] = acc["s"]
        sums_v[q] = acc["v"]
        return carry

    lax.fori_loop(0, last_q + 1, q_body, 0)

    total = red_finish(0)
    for i in range(1, len(phases)):
        red_start(i, total)
        total = red_finish(i)
    totals = jnp.sum(total, axis=1, keepdims=True)
    e0, g1, g2 = totals[0:1], totals[1:2], totals[2:3]
    g3 = totals[3:4] * inv36
    alpha = e0 / g1
    e1 = e0 - 2.0 * alpha * g1 + alpha * alpha * g2
    keep = 1.0 + e1 / e0
    den = keep * keep * g1 - 2.0 * keep * alpha * g2 + alpha * alpha * g3
    alpha1 = e1 / den
    p = alpha + alpha1 * keep
    q = alpha1 * alpha
    for k in range(Z):
        rows = slice(k * Y, (k + 1) * Y)
        x_ref[rows, :] = v_hist[0, rows, :] + p * v_hist[half, rows, :] - q * v_hist[last_q, rows, :]
        r_ref[rows, :] = s_hist[0, rows, :] - p * s_hist[half, rows, :] + q * s_hist[last_q, rows, :]


def body(sizes, right_side, initial, kappa_sq):
    Z, Y, X = right_side.shape
    N = Z * Y
    f32 = jnp.float32
    flat = lambda a: a.reshape(N, X)
    vm = pl.BlockSpec(memory_space=pltpu.VMEM)
    hbm = pl.BlockSpec(memory_space=pltpu.HBM)
    assert 4 * Z == X and Y % 8 == 0
    phases = [("gx", "gy"), ("gz",)] if sizes["gx"] * sizes["gy"] <= 16 else [(a,) for a in AXES]
    groups = [group_size(sizes, axes) for axes in phases] + [1]
    slots = 3
    count = 2 * SWEEPS + 1
    out = pl.pallas_call(
        functools.partial(kernel, sizes, phases, (Z, Y, X)),
        out_shape=[jax.ShapeDtypeStruct((N, X), f32)] * 2,
        in_specs=[hbm] * 3,
        out_specs=[vm] * 2,
        scratch_shapes=[
            pltpu.VMEM((N + 2 * Y, X), f32),
            pltpu.VMEM((N, X), f32),
            pltpu.VMEM((count + 1, N, X), f32),
            pltpu.VMEM((count, N, X), f32),
            pltpu.VMEM((N + 2 * Y, X), f32),
            pltpu.VMEM((2, Z, X), f32),
            pltpu.VMEM((N, X), f32),
            pltpu.VMEM((N, X), f32),
            pltpu.VMEM((slots, 4 * Z + Y, X), f32),
            pltpu.VMEM((slots, 2, Y, X), f32),
            pltpu.VMEM((slots, 2, 2 * Z, X), f32),
            pltpu.VMEM((slots, 2, 2 * Y, X), f32),
            pltpu.VMEM((slots, 2, 2, 8, X), f32),
            pltpu.VMEM((slots, 2, 2, Y, X), f32),
            pltpu.VMEM((slots, 2, 2, 8, X), f32),
            pltpu.VMEM((2, Y, X), f32),
            pltpu.VMEM((2, Z, X), f32),
            pltpu.VMEM((Y, X), f32),
            pltpu.VMEM((count, 8, X), f32),
            pltpu.VMEM((count, 8, X), f32),
            pltpu.VMEM((8, X), f32),
            pltpu.VMEM((3, 8, X), f32),
        ] + [pltpu.VMEM(((groups + [1])[i], 8, X), f32) for i in range(3)] + [
            pltpu.SemaphoreType.DMA((slots, len(DIRECTIONS))),
            pltpu.SemaphoreType.DMA((slots, len(DIRECTIONS))),
            pltpu.SemaphoreType.DMA((3, max(groups))),
            pltpu.SemaphoreType.DMA((3, max(groups))),
            pltpu.SemaphoreType.DMA((3,)),
        ],
        compiler_params=pltpu.CompilerParams(
            collective_id=0, has_side_effects=True, vmem_limit_bytes=63 * 1024 * 1024),
        name="cg",
    )(flat(right_side), flat(initial), flat(kappa_sq))
    return tuple(o.reshape(Z, Y, X) for o in out)


def solution(mesh):
    spec = P("gz", "gy", "gx")
    sizes = {a: mesh.shape[a] for a in AXES}
    return jax.shard_map(functools.partial(body, sizes), mesh=mesh, in_specs=(spec,) * 3,
                         out_specs=(spec,) * 2, check_vma=False)
```

```python
import functools
import jax
import jax.numpy as jnp
from jax import lax
from jax.experimental import pallas as pl
from jax.experimental.pallas import tpu as pltpu
from jax.sharding import PartitionSpec as P

SWEEPS = 3
cheb_high = 7.2
cheb_low = 0.072
MESH = pl.DeviceIdType.MESH
AXES = ("gx", "gy", "gz")
DIRECTIONS = [(z, y, x) for z in (-1, 0, 1) for y in (-1, 0, 1) for x in (-1, 0, 1)
              if 1 <= abs(z) + abs(y) + abs(x) <= 2]


def group_size(sizes, axes):
    size = 1
    for a in axes:
        size *= sizes[a]
    return size


def rank(sizes, where, axes):
    index = 0
    for a in axes:
        index = index * sizes[a] + where[a]
    return index


def peers(sizes, me, axes):
    found = []
    for k in range(1, group_size(sizes, axes)):
        to, origin, left = {}, {}, k
        for a in reversed(axes):
            shift, left = left % sizes[a], left // sizes[a]
            to[a] = lax.rem(me[a] + shift, sizes[a])
            origin[a] = lax.rem(me[a] + sizes[a] - shift, sizes[a])
        found.append((to, origin))
    return found


def sweep_weights():
    centre = (cheb_high + cheb_low) / 2.0
    half_width = (cheb_high - cheb_low) / 2.0
    sigma = centre / half_width
    old = 1.0 / sigma
    weights = []
    for _ in range(SWEEPS - 1):
        new = 1.0 / (2.0 * sigma - old)
        weights.append((new * old, 2.0 * new / half_width))
        old = new
    return 1.0 / centre, weights


def kernel(sizes, phases, shape, b_hbm, x0_hbm, kap_hbm, x_ref, r_ref,
           v_ref, e_ref, u_ref, t_ref, c_ref, d_ref,
           send, xhalo, yhalo, zhalo, zyhalo, zxhalo, yxhalo, cz_ref, cy_ref, cx_ref, cown_ref,
           sums_s, sums_v, part, gather_a, gather_b, gather_c,
           send_sem, recv_sem, red_send, red_recv, in_sem):
    Z, Y, X = shape
    N = Z * Y
    me = {a: lax.axis_index(a) for a in AXES}
    inv_centre, weights = sweep_weights()
    inv36 = 1.0 / 36.0
    half = SWEEPS
    last_q = 2 * half
    zero_slot = last_q + 2

    loads = [pltpu.make_async_copy(kap_hbm, c_ref, in_sem.at[0]),
             pltpu.make_async_copy(x0_hbm, v_ref.at[0, pl.ds(Y, N)], in_sem.at[1]),
             pltpu.make_async_copy(b_hbm, e_ref.at[0], in_sem.at[2])]
    for load in loads:
        load.start()

    for halo in (xhalo, yhalo, zhalo, zyhalo, zxhalo, yxhalo):
        halo[...] = jnp.zeros_like(halo)

    other_x = sizes["gx"] == 2

    def offset(d):
        to = {a: me[a] + s for a, s in zip(("gz", "gy", "gx"), d) if s}
        if other_x and d[2]:
            to["gx"] = 1 - me["gx"]
        return to

    def has(d):
        cond = None
        for a, s in zip(("gz", "gy", "gx"), d):
            if s and not (other_x and a == "gx"):
                one = me[a] > 0 if s < 0 else me[a] < sizes[a] - 1
                cond = one if cond is None else cond & one
        return cond

    def when(cond, fn):
        if cond is None:
            fn()
        else:
            pl.when(cond)(fn)

    DIRS = [d for d in DIRECTIONS
            if all(s == 0 or sizes[a] > 1 for a, s in zip(("gz", "gy", "gx"), d))
            and not (other_x and d[2] < 0)]

    def reverse(d):
        return (-d[0], -d[1], d[2] if other_x else -d[2])

    barrier = pltpu.get_barrier_semaphore()
    count = 0
    for d in DIRS:
        cond = has(d)

        def greet(d=d):
            pl.semaphore_signal(barrier, inc=1, device_id=offset(d), device_id_type=MESH)
        when(cond, greet)
        count = count + (1 if cond is None else jnp.where(cond, 1, 0))
    for axes in phases:
        for peer in peers(sizes, me, axes):
            pl.semaphore_signal(barrier, inc=1, device_id=peer[0], device_id_type=MESH)
            count = count + 1

    guard = jnp.zeros((Y, X), jnp.float32)
    for j in range(last_q + 2):
        v_ref[j, 0:Y, :] = guard
        v_ref[j, Y + N:2 * Y + N, :] = guard
    u_ref[0:Y, :] = guard
    u_ref[Y + N:2 * Y + N, :] = guard
    for k in range(Z):
        e_ref[zero_slot, k * Y:(k + 1) * Y, :] = guard
        d_ref[k * Y:(k + 1) * Y, :] = guard

    lane = lax.broadcasted_iota(jnp.int32, (Y, X), 1)
    row = lax.broadcasted_iota(jnp.int32, (Y, X), 0)
    quarter, place = lane // 4, lane % 4
    left_half = place < 2
    first_x, last_x = lane == 0, lane == X - 1
    edge_x = first_x | last_x
    first_y, last_y = row == 0, row == Y - 1
    lane_z = lax.broadcasted_iota(jnp.int32, (Z, X), 1)
    row_z = lax.broadcasted_iota(jnp.int32, (Z, X), 0)

    at_lo, at_x, at_hi = Z, 2 * Z, 2 * Z + Y

    def pack_y(slot, src, off):
        for at, y in ((0, 1), (at_lo, 0), (at_hi, Y - 1), (at_hi + Z, Y - 2)):
            send[slot, at:at + Z, :] = src[pl.ds(off + y, Z, stride=Y), :]

    def pack_x(slot, src, off):
        acc = jnp.zeros((Y, X), jnp.float32)
        for k in range(Z):
            v = src[off + k * Y:off + (k + 1) * Y, :]
            acc = jnp.where(quarter == k, pltpu.roll(v, (2 + 4 * k) % X, 1), acc)
        send[slot, at_x:at_x + Y, :] = acc

    def source_of(d, slot, src, off):
        dz, dy, dx = d
        out = send.at[slot]
        if dx:
            if dy == 0:
                return out.at[pl.ds(at_x, Y)]
            return out.at[pl.ds(at_lo if dy < 0 else at_x, Z + Y)]
        if dy and dz:
            return out.at[pl.ds((at_lo if dy < 0 else at_hi) + (0 if dz < 0 else Z - 8), 8)]
        if dy:
            return out.at[pl.ds(0 if dy < 0 else at_hi, 2 * Z)]
        return src.at[pl.ds(off if dz < 0 else off + N - 2 * Y, 2 * Y)]

    def halo_of(d, slot, side_x):
        sz, sy = (0 if s > 0 else 1 for s in d[:2])
        sx = side_x if other_x else (0 if d[2] > 0 else 1)
        dz, dy, dx = d
        if dx and dy:
            return yxhalo.at[slot, sy, sx]
        if dx and dz:
            return zxhalo.at[slot, sz, sx]
        if dx:
            return xhalo.at[slot, sx]
        if dy and dz:
            return zyhalo.at[slot, sz, sy]
        return yhalo.at[slot, sy] if dy else zhalo.at[slot, sz]

    def copy_to(d, slot, src, off):
        i = DIRECTIONS.index(d)
        return pltpu.make_async_remote_copy(
            src_ref=source_of(d, slot, src, off), dst_ref=halo_of(d, slot, me["gx"]),
            send_sem=send_sem.at[slot, i], recv_sem=recv_sem.at[slot, i],
            device_id=offset(d), device_id_type=MESH)

    def copy_from(d, slot, src, off):
        back = reverse(d)
        i = DIRECTIONS.index(back)
        return pltpu.make_async_remote_copy(
            src_ref=source_of(back, slot, src, off), dst_ref=halo_of(back, slot, 1 - me["gx"]),
            send_sem=send_sem.at[slot, i], recv_sem=recv_sem.at[slot, i],
            device_id=offset(d), device_id_type=MESH)

    def start_all(slot, src, off, packed_x=False):
        def go(want):
            for d in DIRS:
                if want(d):
                    when(has(d), lambda d=d: copy_to(d, slot, src, off).start())

        if packed_x:
            go(lambda d: d[2] != 0 and d[1] == 0)
        pack_y(slot, src, off)
        if packed_x:
            go(lambda d: d[2] != 0 and d[1] != 0)
        go(lambda d: d[0] != 0 and d[1] != 0 and d[2] == 0)
        go(lambda d: d[1] != 0 and d[0] == 0 and d[2] == 0)
        go(lambda d: d[0] != 0 and d[1] == 0 and d[2] == 0)
        if not packed_x:
            pack_x(slot, src, off)
            go(lambda d: d[2] != 0)

    def finish(edges, slot, src, off):
        for d in DIRS:
            if (sum(1 for s in d if s) > 1) != edges:
                continue

            def done(d=d):
                copy_from(d, slot, src, off).wait_recv()
                copy_to(d, slot, src, off).wait_send()
            when(has(d), done)

    def faces(slot):
        z1 = [zhalo[slot, 0, Y:2 * Y, :], zhalo[slot, 1, 0:Y, :]]
        y1 = [yhalo[slot, 0, 0:Z, :], yhalo[slot, 1, Z:2 * Z, :]]
        x1 = jnp.where(left_half, xhalo[slot, 0], xhalo[slot, 1])
        return z1, y1, x1

    def pairs_of(columns):
        return jnp.where(place == 2, pltpu.roll(columns, 1, 1), pltpu.roll(columns, X - 1, 1))

    def edge_of(pairs, k):
        return jnp.where(edge_x, pltpu.roll(pairs, (2 * X - 2 - 4 * k) % X, 1), 0.0)

    def along_x(v, lanes):
        return (jnp.where(lanes == 0, 0.0, pltpu.roll(v, 1, 1))
                + jnp.where(lanes == X - 1, 0.0, pltpu.roll(v, X - 1, 1)))

    exists = {a: [jnp.where(me[a] > 0, 1.0, 0.0).astype(jnp.float32),
                  jnp.where(me[a] < sizes[a] - 1, 1.0, 0.0).astype(jnp.float32)] for a in AXES}

    def outer(slot, v, off):
        z1, y1, x1 = faces(slot)
        z2 = [zhalo[slot, 0, 0:Y, :], zhalo[slot, 1, Y:2 * Y, :]]
        y2 = [yhalo[slot, 0, Z:2 * Z, :], yhalo[slot, 1, 0:Z, :]]
        zx = [jnp.where(left_half, zxhalo[slot, s, 0], zxhalo[slot, s, 1]) for s in (0, 1)]
        yx = [jnp.where(left_half, yxhalo[slot, s, 0, r:r + Y, :], yxhalo[slot, s, 1, r:r + Y, :])
              for s, r in ((0, 0), (1, Z))]
        zy = [[zyhalo[slot, sz, sy, r:r + 1, :] for sy in (0, 1)] for sz, r in ((0, 7), (1, 0))]
        uz, uy = [], []
        for s, k in ((0, 0), (1, Z - 1)):
            f = z1[s]
            total = z2[s] + v[off + k * Y:off + (k + 1) * Y, :] + along_x(f, lane)
            total = total + edge_of(pairs_of(zx[s]), Z - 1 - k)
            total = total + jnp.where(first_y, zy[s][0], pltpu.roll(f, 1, 0))
            total = total + jnp.where(last_y, zy[s][1], pltpu.roll(f, Y - 1, 0))
            uz.append((cz_ref[s] * f - total) * exists["gz"][s])
        for s, at, r in ((0, at_lo, Y), (1, at_hi, 0)):
            f = y1[s]
            total = y2[s] + send[slot, at:at + Z, :]
            total = total + jnp.where(lane_z == 0, pltpu.roll(yxhalo[slot, s, 0, r:r + Z, :], 1, 1),
                                      pltpu.roll(f, 1, 1))
            total = total + jnp.where(lane_z == X - 1,
                                      pltpu.roll(yxhalo[slot, s, 1, r:r + Z, :], X - 1, 1),
                                      pltpu.roll(f, X - 1, 1))
            total = total + jnp.where(row_z == 0, zy[0][s], pltpu.roll(f, 1, 0))
            total = total + jnp.where(row_z == Z - 1, zy[1][s], pltpu.roll(f, Z - 1, 0))
            uy.append((cy_ref[s] * f - total) * exists["gy"][s])
        own = send[slot, at_x:at_x + Y, :]
        total = jnp.where(place == 1, pltpu.roll(x1, 1, 1) + pltpu.roll(own, X - 1, 1),
                          pltpu.roll(x1, X - 1, 1) + pltpu.roll(own, 1, 1))
        total = total + jnp.where(first_y, yx[0][Y - 1:Y, :], pltpu.roll(x1, 1, 0))
        total = total + jnp.where(last_y, yx[1][0:1, :], pltpu.roll(x1, Y - 1, 0))
        total = total + jnp.where(lane < 4, pltpu.roll(zx[0], 4, 1), pltpu.roll(x1, 4, 1))
        total = total + jnp.where(lane >= X - 4, pltpu.roll(zx[1], X - 4, 1),
                                  pltpu.roll(x1, X - 4, 1))
        ux = (cx_ref[...] * x1 - total) * jnp.where(left_half, exists["gx"][0], exists["gx"][1])
        return uz, uy, ux

    def k_inner(src, dst, dst_off):
        for k in range(Z):
            i = Y + k * Y
            v = src[i:i + Y, :]
            total = src[i - Y:i, :] + src[i + Y:i + 2 * Y, :] + along_x(v, lane)
            total = total + jnp.where(first_y, 0.0, src[i - 1:i - 1 + Y, :])
            total = total + jnp.where(last_y, 0.0, src[i + 1:i + 1 + Y, :])
            dst[dst_off + k * Y:dst_off + (k + 1) * Y, :] = c_ref[k * Y:(k + 1) * Y, :] * v - total

    def k_edges(halo, beyond):
        for s, k, inward in ((0, 0, 1), (1, Z - 1, Z - 2)):
            f = halo[0][s]
            rows = slice(k * Y, (k + 1) * Y)
            t_ref[rows, :] = (t_ref[rows, :] - beyond[0][s] - c_ref[rows, :] * f + along_x(f, lane)
                              + jnp.where(first_y, 0.0, pltpu.roll(f, 1, 0))
                              + jnp.where(last_y, 0.0, pltpu.roll(f, Y - 1, 0)))
            rows = slice(inward * Y, (inward + 1) * Y)
            t_ref[rows, :] = t_ref[rows, :] + f
        for s, y, inward in ((0, 0, 1), (1, Y - 1, Y - 2)):
            f = halo[1][s]
            rows = pl.ds(y, Z, stride=Y)
            t_ref[rows, :] = (t_ref[rows, :] - beyond[1][s] - c_ref[rows, :] * f + along_x(f, lane_z)
                              + jnp.where(row_z == 0, 0.0, pltpu.roll(f, 1, 0))
                              + jnp.where(row_z == Z - 1, 0.0, pltpu.roll(f, Z - 1, 0)))
            rows = pl.ds(inward, Z, stride=Y)
            t_ref[rows, :] = t_ref[rows, :] + f
        f = pairs_of(halo[2])
        edge = (-pairs_of(beyond[2]) - cown_ref[...] * f
                + jnp.where(first_y, 0.0, pltpu.roll(f, 1, 0))
                + jnp.where(last_y, 0.0, pltpu.roll(f, Y - 1, 0))
                + jnp.where(lane < 4, 0.0, pltpu.roll(f, 4, 1))
                + jnp.where(lane >= X - 4, 0.0, pltpu.roll(f, X - 4, 1)))
        return jnp.where(place == 3, pltpu.roll(f, 1, 1),
                         jnp.where(place == 0, pltpu.roll(f, X - 1, 1), edge))

    two_x = (lane < 2) | (lane >= X - 2)

    loads[0].wait()
    pl.semaphore_wait(barrier, count)
    start_all(2, c_ref, 0)
    loads[1].wait()
    start_all(0, v_ref.at[0], Y)
    loads[2].wait()
    finish(False, 2, c_ref, 0)
    finish(True, 2, c_ref, 0)
    kz, ky, kx = faces(2)
    for s in (0, 1):
        cz_ref[s] = 6.0 + kz[s]
        cy_ref[s] = 6.0 + ky[s]
    cx_ref[...] = 6.0 + kx
    cown_ref[...] = 6.0 + send[2, at_x:at_x + Y, :]
    for k in range(Z):
        rows = slice(k * Y, (k + 1) * Y)
        c_ref[rows, :] = 6.0 + c_ref[rows, :]

    gathers = (gather_a, gather_b, gather_c)

    def red_start(i, value):
        part[i] = value
        gathers[i][pl.ds(rank(sizes, me, phases[i]), 1)] = value[None]
        for k, (peer, _) in enumerate(peers(sizes, me, phases[i])):
            pltpu.make_async_remote_copy(
                src_ref=part.at[i], dst_ref=gathers[i].at[rank(sizes, me, phases[i])],
                send_sem=red_send.at[i, k], recv_sem=red_recv.at[i, k],
                device_id=peer, device_id_type=MESH).start()

    def red_finish(i):
        for k, (peer, origin) in enumerate(peers(sizes, me, phases[i])):
            copy = pltpu.make_async_remote_copy(
                src_ref=part.at[i], dst_ref=gathers[i].at[rank(sizes, origin, phases[i])],
                send_sem=red_send.at[i, k], recv_sem=red_recv.at[i, k],
                device_id=peer, device_id_type=MESH)
            copy.wait_recv()
            copy.wait_send()
        total = gathers[i][0]
        for j in range(1, group_size(sizes, phases[i])):
            total = total + gathers[i][j]
        return total

    def red_first():
        rows8 = lax.broadcasted_iota(jnp.int32, (8, X), 0)
        mine = jnp.zeros((8, X), jnp.float32)
        for j, value in enumerate((sums_s[half - 1], sums_v[half], sums_s[last_q - 1], sums_v[last_q])):
            mine = jnp.where(rows8 == j, jnp.sum(value, axis=0, keepdims=True), mine)
        red_start(0, mine)

    def q_body(q, carry):
        phase = lax.rem(q, half)
        sweep = jnp.minimum(phase, 1)
        source = sweep * (1 + half * (q // half)) + (1 - sweep) * zero_slot * ((q + last_q - 1) // last_q)
        sign = jnp.where((sweep == 0) & (q > 0), -1.0, 1.0).astype(jnp.float32)
        old, new, keep = jnp.float32(0.0), sign * jnp.float32(inv_centre), jnp.float32(0.0)
        for j, (wo, wn) in enumerate(weights):
            old = jnp.where(phase == j + 1, jnp.float32(wo), old)
            new = jnp.where(phase == j + 1, jnp.float32(wn), new)
            keep = jnp.where(phase == j + 1, jnp.float32(1.0), keep)
        v = v_ref.at[q]
        v_new = v_ref.at[q + 1]
        zero8 = jnp.zeros((8, X), jnp.float32)
        acc = {"s": zero8, "v": zero8, "x": jnp.zeros((Y, X), jnp.float32)}

        def fold(name, value):
            for j in range(0, Y, 8):
                acc[name] = acc[name] + value[j:j + 8]

        def post_t(k, t):
            rows = slice(k * Y, (k + 1) * Y)
            vrows = slice(Y + k * Y, 2 * Y + k * Y)
            t = t * inv36
            src = e_ref[source, rows, :]
            defect = src - t
            e_ref[q + 1, rows, :] = sign * defect
            upd = old * d_ref[rows, :] + new * defect
            d_ref[rows, :] = upd
            was = v[vrows, :]
            z = keep * was + upd
            v_new[vrows, :] = z
            fold("s", src * z)
            fold("v", was * t)
            acc["x"] = jnp.where(quarter == k, pltpu.roll(z, (2 + 4 * k) % X, 1), acc["x"])

        slot = lax.rem(q, 2)
        k_inner(v, u_ref, Y)
        k_inner(u_ref, t_ref, 0)
        finish(False, slot, v, Y)
        finish(True, slot, v, Y)
        columns = k_edges(faces(slot), outer(slot, v, Y))
        for k in range(Z):
            fix = jnp.where(two_x, pltpu.roll(columns, (2 * X - 2 - 4 * k) % X, 1), 0.0)
            post_t(k, t_ref[k * Y:(k + 1) * Y, :] + fix)
        send[1 - slot, at_x:at_x + Y, :] = acc["x"]
        pl.when(q < last_q)(lambda: start_all(1 - slot, v_new, Y, packed_x=True))
        sums_s[q] = acc["s"]
        sums_v[q] = acc["v"]
        return carry

    lax.fori_loop(0, last_q + 1, q_body, 0)

    red_first()
    total = red_finish(0)
    for i in range(1, len(phases)):
        red_start(i, total)
        total = red_finish(i)
    totals = jnp.sum(total, axis=1, keepdims=True)
    e0, g1, g2 = totals[0:1], totals[1:2], totals[2:3]
    g3 = totals[3:4]
    alpha = e0 / g1
    e1 = e0 - 2.0 * alpha * g1 + alpha * alpha * g2
    keep = 1.0 + e1 / e0
    den = keep * keep * g1 - 2.0 * keep * alpha * g2 + alpha * alpha * g3
    alpha1 = e1 / den
    p = alpha + alpha1 * keep
    q = alpha1 * alpha
    for k in range(Z):
        rows = slice(k * Y, (k + 1) * Y)
        vrows = slice(Y + k * Y, 2 * Y + k * Y)
        x_ref[rows, :] = v_ref[0, vrows, :] + p * v_ref[half, vrows, :] - q * v_ref[last_q, vrows, :]
        r_ref[rows, :] = e_ref[1, rows, :] - p * e_ref[half + 1, rows, :] + q * e_ref[last_q + 1, rows, :]


def body(sizes, right_side, initial, kappa_sq):
    Z, Y, X = right_side.shape
    N = Z * Y
    f32 = jnp.float32
    flat = lambda a: a.reshape(N, X)
    vm = pl.BlockSpec(memory_space=pltpu.VMEM)
    hbm = pl.BlockSpec(memory_space=pltpu.HBM)
    assert 4 * Z == X and Y % 8 == 0
    phases = [("gx", "gy"), ("gz",)] if sizes["gx"] * sizes["gy"] <= 16 else [(a,) for a in AXES]
    groups = [group_size(sizes, axes) for axes in phases] + [1]
    slots = 3
    count = 2 * SWEEPS + 1
    out = pl.pallas_call(
        functools.partial(kernel, sizes, phases, (Z, Y, X)),
        out_shape=[jax.ShapeDtypeStruct((N, X), f32)] * 2,
        in_specs=[hbm] * 3,
        out_specs=[vm] * 2,
        scratch_shapes=[
            pltpu.VMEM((count + 1, N + 2 * Y, X), f32),
            pltpu.VMEM((count + 2, N, X), f32),
            pltpu.VMEM((N + 2 * Y, X), f32),
            pltpu.VMEM((N, X), f32),
            pltpu.VMEM((N, X), f32),
            pltpu.VMEM((N, X), f32),
            pltpu.VMEM((slots, 4 * Z + Y, X), f32),
            pltpu.VMEM((slots, 2, Y, X), f32),
            pltpu.VMEM((slots, 2, 2 * Z, X), f32),
            pltpu.VMEM((slots, 2, 2 * Y, X), f32),
            pltpu.VMEM((slots, 2, 2, 8, X), f32),
            pltpu.VMEM((slots, 2, 2, Y, X), f32),
            pltpu.VMEM((slots, 2, 2, Z + Y, X), f32),
            pltpu.VMEM((2, Y, X), f32),
            pltpu.VMEM((2, Z, X), f32),
            pltpu.VMEM((Y, X), f32),
            pltpu.VMEM((Y, X), f32),
            pltpu.VMEM((count, 8, X), f32),
            pltpu.VMEM((count, 8, X), f32),
            pltpu.VMEM((3, 8, X), f32),
        ] + [pltpu.VMEM(((groups + [1])[i], 8, X), f32) for i in range(3)] + [
            pltpu.SemaphoreType.DMA((slots, len(DIRECTIONS))),
            pltpu.SemaphoreType.DMA((slots, len(DIRECTIONS))),
            pltpu.SemaphoreType.DMA((3, max(groups))),
            pltpu.SemaphoreType.DMA((3, max(groups))),
            pltpu.SemaphoreType.DMA((3,)),
        ],
        compiler_params=pltpu.CompilerParams(
            collective_id=0, has_side_effects=True, vmem_limit_bytes=63 * 1024 * 1024),
        name="cg",
    )(flat(right_side), flat(initial), flat(kappa_sq))
    return tuple(o.reshape(Z, Y, X) for o in out)


def solution(mesh):
    spec = P("gz", "gy", "gx")
    sizes = {a: mesh.shape[a] for a in AXES}
    return jax.shard_map(functools.partial(body, sizes), mesh=mesh, in_specs=(spec,) * 3,
                         out_specs=(spec,) * 2, check_vma=False)
```

```python
import functools
import jax
import jax.numpy as jnp
from jax import lax
from jax.experimental import pallas as pl
from jax.experimental.pallas import tpu as pltpu
from jax.sharding import PartitionSpec as P

SWEEPS = 3
cheb_high = 7.2
cheb_low = 0.072
MESH = pl.DeviceIdType.MESH
AXES = ("gx", "gy", "gz")
DIRECTIONS = [(z, y, x) for z in (-1, 0, 1) for y in (-1, 0, 1) for x in (-1, 0, 1)
              if 1 <= abs(z) + abs(y) + abs(x) <= 2]


def group_size(sizes, axes):
    size = 1
    for a in axes:
        size *= sizes[a]
    return size


def rank(sizes, where, axes):
    index = 0
    for a in axes:
        index = index * sizes[a] + where[a]
    return index


def peers(sizes, me, axes):
    found = []
    for k in range(1, group_size(sizes, axes)):
        to, origin, left = {}, {}, k
        for a in reversed(axes):
            shift, left = left % sizes[a], left // sizes[a]
            to[a] = lax.rem(me[a] + shift, sizes[a])
            origin[a] = lax.rem(me[a] + sizes[a] - shift, sizes[a])
        found.append((to, origin))
    return found


def sweep_weights():
    centre = (cheb_high + cheb_low) / 2.0
    half_width = (cheb_high - cheb_low) / 2.0
    sigma = centre / half_width
    old = 1.0 / sigma
    weights = []
    for _ in range(SWEEPS - 1):
        new = 1.0 / (2.0 * sigma - old)
        weights.append((new * old, 2.0 * new / half_width))
        old = new
    return 1.0 / centre, weights


def kernel(sizes, phases, shape, b_hbm, x0_hbm, kap_hbm, x_ref, r_ref,
           v_ref, e_ref, u_ref, t_ref, c_ref, d_ref,
           send, xhalo, yhalo, zhalo, zyhalo, zxhalo, yxhalo, cz_ref, cy_ref, cx_ref,
           sums_s, sums_v, part, gather_a, gather_b, gather_c,
           send_sem, recv_sem, red_send, red_recv, in_sem):
    Z, Y, X = shape
    N = Z * Y
    me = {a: lax.axis_index(a) for a in AXES}
    inv_centre, weights = sweep_weights()
    inv36 = 1.0 / 36.0
    half = SWEEPS
    last_q = 2 * half
    zero_slot = last_q + 2

    loads = [pltpu.make_async_copy(kap_hbm, c_ref, in_sem.at[0]),
             pltpu.make_async_copy(x0_hbm, v_ref.at[0, pl.ds(Y, N)], in_sem.at[1]),
             pltpu.make_async_copy(b_hbm, e_ref.at[0], in_sem.at[2])]
    for load in loads:
        load.start()

    for halo in (xhalo, yhalo, zhalo, zyhalo, zxhalo, yxhalo):
        halo[...] = jnp.zeros_like(halo)

    other_x = sizes["gx"] == 2

    def offset(d):
        to = {a: me[a] + s for a, s in zip(("gz", "gy", "gx"), d) if s}
        if other_x and d[2]:
            to["gx"] = 1 - me["gx"]
        return to

    def has(d):
        cond = None
        for a, s in zip(("gz", "gy", "gx"), d):
            if s and not (other_x and a == "gx"):
                one = me[a] > 0 if s < 0 else me[a] < sizes[a] - 1
                cond = one if cond is None else cond & one
        return cond

    def when(cond, fn):
        if cond is None:
            fn()
        else:
            pl.when(cond)(fn)

    DIRS = [d for d in DIRECTIONS
            if all(s == 0 or sizes[a] > 1 for a, s in zip(("gz", "gy", "gx"), d))
            and not (other_x and d[2] < 0)]

    def reverse(d):
        return (-d[0], -d[1], d[2] if other_x else -d[2])

    barrier = pltpu.get_barrier_semaphore()
    count = 0
    for d in DIRS:
        cond = has(d)

        def greet(d=d):
            pl.semaphore_signal(barrier, inc=1, device_id=offset(d), device_id_type=MESH)
        when(cond, greet)
        count = count + (1 if cond is None else jnp.where(cond, 1, 0))
    for axes in phases:
        for peer in peers(sizes, me, axes):
            pl.semaphore_signal(barrier, inc=1, device_id=peer[0], device_id_type=MESH)
            count = count + 1

    guard = jnp.zeros((Y, X), jnp.float32)
    for j in range(last_q + 2):
        v_ref[j, 0:Y, :] = guard
        v_ref[j, Y + N:2 * Y + N, :] = guard
    u_ref[0:Y, :] = guard
    u_ref[Y + N:2 * Y + N, :] = guard
    for k in range(Z):
        e_ref[zero_slot, k * Y:(k + 1) * Y, :] = guard
        d_ref[k * Y:(k + 1) * Y, :] = guard

    lane = lax.broadcasted_iota(jnp.int32, (Y, X), 1)
    row = lax.broadcasted_iota(jnp.int32, (Y, X), 0)
    quarter, place = lane // 4, lane % 4
    left_half = place < 2
    first_x, last_x = lane == 0, lane == X - 1
    edge_x = first_x | last_x
    first_y, last_y = row == 0, row == Y - 1
    lane_z = lax.broadcasted_iota(jnp.int32, (Z, X), 1)
    row_z = lax.broadcasted_iota(jnp.int32, (Z, X), 0)

    at_lo, at_x, at_hi = Z, 2 * Z, 2 * Z + Y

    def pack_y(slot, src, off):
        for at, y in ((0, 1), (at_lo, 0), (at_hi, Y - 1), (at_hi + Z, Y - 2)):
            send[slot, at:at + Z, :] = src[pl.ds(off + y, Z, stride=Y), :]

    def pack_x(slot, src, off):
        acc = jnp.zeros((Y, X), jnp.float32)
        for k in range(Z):
            v = src[off + k * Y:off + (k + 1) * Y, :]
            acc = jnp.where(quarter == k, pltpu.roll(v, (2 + 4 * k) % X, 1), acc)
        send[slot, at_x:at_x + Y, :] = acc

    def source_of(d, slot, src, off):
        dz, dy, dx = d
        out = send.at[slot]
        if dx:
            if dy == 0:
                return out.at[pl.ds(at_x, Y)]
            return out.at[pl.ds(at_x if dy < 0 else at_x + Y - 8, 8)]
        if dy and dz:
            return out.at[pl.ds((at_lo if dy < 0 else at_hi) + (0 if dz < 0 else Z - 8), 8)]
        if dy:
            return out.at[pl.ds(0 if dy < 0 else at_hi, 2 * Z)]
        return src.at[pl.ds(off if dz < 0 else off + N - 2 * Y, 2 * Y)]

    def halo_of(d, slot, side_x):
        sz, sy = (0 if s > 0 else 1 for s in d[:2])
        sx = side_x if other_x else (0 if d[2] > 0 else 1)
        dz, dy, dx = d
        if dx and dy:
            return yxhalo.at[slot, sy, sx]
        if dx and dz:
            return zxhalo.at[slot, sz, sx]
        if dx:
            return xhalo.at[slot, sx]
        if dy and dz:
            return zyhalo.at[slot, sz, sy]
        return yhalo.at[slot, sy] if dy else zhalo.at[slot, sz]

    def copy_to(d, slot, src, off):
        i = DIRECTIONS.index(d)
        return pltpu.make_async_remote_copy(
            src_ref=source_of(d, slot, src, off), dst_ref=halo_of(d, slot, me["gx"]),
            send_sem=send_sem.at[slot, i], recv_sem=recv_sem.at[slot, i],
            device_id=offset(d), device_id_type=MESH)

    def copy_from(d, slot, src, off):
        back = reverse(d)
        i = DIRECTIONS.index(back)
        return pltpu.make_async_remote_copy(
            src_ref=source_of(back, slot, src, off), dst_ref=halo_of(back, slot, 1 - me["gx"]),
            send_sem=send_sem.at[slot, i], recv_sem=recv_sem.at[slot, i],
            device_id=offset(d), device_id_type=MESH)

    def start_all(slot, src, off, packed_x=False, edges=True):
        def go(want):
            for d in DIRS:
                if want(d) and (edges or sum(1 for s in d if s) == 1):
                    when(has(d), lambda d=d: copy_to(d, slot, src, off).start())

        if packed_x:
            go(lambda d: d[2] != 0 and d[1] == 0)
        pack_y(slot, src, off)
        if packed_x:
            go(lambda d: d[2] != 0 and d[1] != 0)
        go(lambda d: d[0] != 0 and d[1] != 0 and d[2] == 0)
        go(lambda d: d[1] != 0 and d[0] == 0 and d[2] == 0)
        go(lambda d: d[0] != 0 and d[1] == 0 and d[2] == 0)
        if not packed_x:
            pack_x(slot, src, off)
            go(lambda d: d[2] != 0)

    def finish(edges, slot, src, off):
        for d in DIRS:
            if (sum(1 for s in d if s) > 1) != edges:
                continue

            def done(d=d):
                copy_from(d, slot, src, off).wait_recv()
                copy_to(d, slot, src, off).wait_send()
            when(has(d), done)

    def faces(slot):
        z1 = [zhalo[slot, 0, Y:2 * Y, :], zhalo[slot, 1, 0:Y, :]]
        y1 = [yhalo[slot, 0, 0:Z, :], yhalo[slot, 1, Z:2 * Z, :]]
        x1 = jnp.where(left_half, xhalo[slot, 0], xhalo[slot, 1])
        return z1, y1, x1

    def pairs_of(columns):
        return jnp.where(place[0:columns.shape[0]] == 2,
                         pltpu.roll(columns, 1, 1), pltpu.roll(columns, X - 1, 1))

    def along_x(v, lanes):
        return (jnp.where(lanes == 0, 0.0, pltpu.roll(v, 1, 1))
                + jnp.where(lanes == X - 1, 0.0, pltpu.roll(v, X - 1, 1)))

    exists = {a: [jnp.where(me[a] > 0, 1.0, 0.0).astype(jnp.float32),
                  jnp.where(me[a] < sizes[a] - 1, 1.0, 0.0).astype(jnp.float32)] for a in AXES}

    def along_y(f):
        return (jnp.where(first_y, 0.0, pltpu.roll(f, 1, 0))
                + jnp.where(last_y, 0.0, pltpu.roll(f, Y - 1, 0)))

    def k_inner(src, dst, dst_off):
        for k in range(Z):
            i = Y + k * Y
            v = src[i:i + Y, :]
            total = src[i - Y:i, :] + src[i + Y:i + 2 * Y, :] + along_x(v, lane)
            total = total + jnp.where(first_y, 0.0, src[i - 1:i - 1 + Y, :])
            total = total + jnp.where(last_y, 0.0, src[i + 1:i + 1 + Y, :])
            dst[dst_off + k * Y:dst_off + (k + 1) * Y, :] = c_ref[k * Y:(k + 1) * Y, :] * v - total

    def k_edges(slot, v, off):
        z1, y1, x1 = faces(slot)
        z2 = [zhalo[slot, 0, 0:Y, :], zhalo[slot, 1, Y:2 * Y, :]]
        y2 = [yhalo[slot, 0, Z:2 * Z, :], yhalo[slot, 1, 0:Z, :]]
        zx = [pairs_of(jnp.where(left_half, zxhalo[slot, s, 0], zxhalo[slot, s, 1])) for s in (0, 1)]
        yx = [pairs_of(jnp.where(left_half[0:8], yxhalo[slot, s, 0], yxhalo[slot, s, 1]))
              for s in (0, 1)]
        zy = [[zyhalo[slot, sz, sy, r:r + 1, :] for sy in (0, 1)] for sz, r in ((0, 7), (1, 0))]
        for s, k, inward in ((0, 0, 1), (1, Z - 1, Z - 2)):
            f = z1[s]
            rows = slice(k * Y, (k + 1) * Y)
            own = v[off + k * Y:off + (k + 1) * Y, :] * exists["gz"][s]
            side = along_x(f, lane) + along_y(f)
            t_ref[rows, :] = t_ref[rows, :] + (z2[s] + own + 2.0 * side - cz_ref[s] * f)
            rows = slice(inward * Y, (inward + 1) * Y)
            t_ref[rows, :] = t_ref[rows, :] + f
        for s, y, inward, at in ((0, 0, 1, at_lo), (1, Y - 1, Y - 2, at_hi)):
            f = y1[s]
            rows = pl.ds(y, Z, stride=Y)
            own = send[slot, at:at + Z, :] * exists["gy"][s]
            side = along_x(f, lane_z)
            side = side + jnp.where(row_z == 0, zy[0][s], pltpu.roll(f, 1, 0))
            side = side + jnp.where(row_z == Z - 1, zy[1][s], pltpu.roll(f, Z - 1, 0))
            t_ref[rows, :] = t_ref[rows, :] + (y2[s] + own + 2.0 * side - cy_ref[s] * f)
            rows = pl.ds(inward, Z, stride=Y)
            t_ref[rows, :] = t_ref[rows, :] + f
        f = pairs_of(x1)
        x2 = jnp.where(place == 2, pltpu.roll(x1, 2, 1), pltpu.roll(x1, X - 2, 1))
        own = send[slot, at_x:at_x + Y, :] * jnp.where(place == 2, exists["gx"][0], exists["gx"][1])
        side = jnp.where(first_y, yx[0][7:8, :], pltpu.roll(f, 1, 0))
        side = side + jnp.where(last_y, yx[1][0:1, :], pltpu.roll(f, Y - 1, 0))
        side = side + jnp.where(lane < 4, pltpu.roll(zx[0], 4, 1), pltpu.roll(f, 4, 1))
        side = side + jnp.where(lane >= X - 4, pltpu.roll(zx[1], X - 4, 1), pltpu.roll(f, X - 4, 1))
        edge = x2 + own + 2.0 * side - cx_ref[...] * f
        return jnp.where(place == 3, pltpu.roll(f, 1, 1),
                         jnp.where(place == 0, pltpu.roll(f, X - 1, 1), edge))

    two_x = (lane < 2) | (lane >= X - 2)

    loads[0].wait()
    pl.semaphore_wait(barrier, count)
    start_all(2, c_ref, 0, edges=False)
    loads[1].wait()
    start_all(0, v_ref.at[0], Y)
    loads[2].wait()
    finish(False, 2, c_ref, 0)
    kz, ky, kx = faces(2)
    for s, k, at in ((0, 0, at_lo), (1, Z - 1, at_hi)):
        cz_ref[s] = 12.0 + kz[s] + c_ref[k * Y:(k + 1) * Y, :]
        cy_ref[s] = 12.0 + ky[s] + send[2, at:at + Z, :]
    cx_ref[...] = 12.0 + pairs_of(kx) + send[2, at_x:at_x + Y, :]
    for k in range(Z):
        rows = slice(k * Y, (k + 1) * Y)
        c_ref[rows, :] = 6.0 + c_ref[rows, :]

    gathers = (gather_a, gather_b, gather_c)

    def red_start(i, value):
        part[i] = value
        gathers[i][pl.ds(rank(sizes, me, phases[i]), 1)] = value[None]
        for k, (peer, _) in enumerate(peers(sizes, me, phases[i])):
            pltpu.make_async_remote_copy(
                src_ref=part.at[i], dst_ref=gathers[i].at[rank(sizes, me, phases[i])],
                send_sem=red_send.at[i, k], recv_sem=red_recv.at[i, k],
                device_id=peer, device_id_type=MESH).start()

    def red_finish(i):
        for k, (peer, origin) in enumerate(peers(sizes, me, phases[i])):
            copy = pltpu.make_async_remote_copy(
                src_ref=part.at[i], dst_ref=gathers[i].at[rank(sizes, origin, phases[i])],
                send_sem=red_send.at[i, k], recv_sem=red_recv.at[i, k],
                device_id=peer, device_id_type=MESH)
            copy.wait_recv()
            copy.wait_send()
        total = gathers[i][0]
        for j in range(1, group_size(sizes, phases[i])):
            total = total + gathers[i][j]
        return total

    def red_first():
        rows8 = lax.broadcasted_iota(jnp.int32, (8, X), 0)
        mine = jnp.zeros((8, X), jnp.float32)
        for j, value in enumerate((sums_s[half - 1], sums_v[half], sums_s[last_q - 1], sums_v[last_q])):
            mine = jnp.where(rows8 == j, jnp.sum(value, axis=0, keepdims=True), mine)
        red_start(0, mine)

    def q_body(q, carry):
        phase = lax.rem(q, half)
        sweep = jnp.minimum(phase, 1)
        source = sweep * (1 + half * (q // half)) + (1 - sweep) * zero_slot * ((q + last_q - 1) // last_q)
        sign = jnp.where((sweep == 0) & (q > 0), -1.0, 1.0).astype(jnp.float32)
        old, new, keep = jnp.float32(0.0), sign * jnp.float32(inv_centre), jnp.float32(0.0)
        for j, (wo, wn) in enumerate(weights):
            old = jnp.where(phase == j + 1, jnp.float32(wo), old)
            new = jnp.where(phase == j + 1, jnp.float32(wn), new)
            keep = jnp.where(phase == j + 1, jnp.float32(1.0), keep)
        v = v_ref.at[q]
        v_new = v_ref.at[q + 1]
        zero8 = jnp.zeros((8, X), jnp.float32)
        acc = {"s": zero8, "v": zero8, "x": jnp.zeros((Y, X), jnp.float32)}

        def fold(name, value):
            for j in range(0, Y, 8):
                acc[name] = acc[name] + value[j:j + 8]

        def post_t(k, t):
            rows = slice(k * Y, (k + 1) * Y)
            vrows = slice(Y + k * Y, 2 * Y + k * Y)
            t = t * inv36
            src = e_ref[source, rows, :]
            defect = src - t
            e_ref[q + 1, rows, :] = sign * defect
            upd = old * d_ref[rows, :] + new * defect
            d_ref[rows, :] = upd
            was = v[vrows, :]
            z = keep * was + upd
            v_new[vrows, :] = z
            fold("s", src * z)
            fold("v", was * t)
            acc["x"] = jnp.where(quarter == k, pltpu.roll(z, (2 + 4 * k) % X, 1), acc["x"])

        slot = lax.rem(q, 2)
        k_inner(v, u_ref, Y)
        k_inner(u_ref, t_ref, 0)
        finish(False, slot, v, Y)
        finish(True, slot, v, Y)
        columns = k_edges(slot, v, Y)
        for k in range(Z):
            fix = jnp.where(two_x, pltpu.roll(columns, (2 * X - 2 - 4 * k) % X, 1), 0.0)
            post_t(k, t_ref[k * Y:(k + 1) * Y, :] + fix)
        send[1 - slot, at_x:at_x + Y, :] = acc["x"]
        pl.when(q < last_q)(lambda: start_all(1 - slot, v_new, Y, packed_x=True))
        sums_s[q] = acc["s"]
        sums_v[q] = acc["v"]
        return carry

    lax.fori_loop(0, last_q + 1, q_body, 0)

    red_first()
    total = red_finish(0)
    for i in range(1, len(phases)):
        red_start(i, total)
        total = red_finish(i)
    totals = jnp.sum(total, axis=1, keepdims=True)
    e0, g1, g2 = totals[0:1], totals[1:2], totals[2:3]
    g3 = totals[3:4]
    alpha = e0 / g1
    e1 = e0 - 2.0 * alpha * g1 + alpha * alpha * g2
    keep = 1.0 + e1 / e0
    den = keep * keep * g1 - 2.0 * keep * alpha * g2 + alpha * alpha * g3
    alpha1 = e1 / den
    p = alpha + alpha1 * keep
    q = alpha1 * alpha
    for k in range(Z):
        rows = slice(k * Y, (k + 1) * Y)
        vrows = slice(Y + k * Y, 2 * Y + k * Y)
        x_ref[rows, :] = v_ref[0, vrows, :] + p * v_ref[half, vrows, :] - q * v_ref[last_q, vrows, :]
        r_ref[rows, :] = e_ref[1, rows, :] - p * e_ref[half + 1, rows, :] + q * e_ref[last_q + 1, rows, :]


def body(sizes, right_side, initial, kappa_sq):
    Z, Y, X = right_side.shape
    N = Z * Y
    f32 = jnp.float32
    flat = lambda a: a.reshape(N, X)
    vm = pl.BlockSpec(memory_space=pltpu.VMEM)
    hbm = pl.BlockSpec(memory_space=pltpu.HBM)
    assert 4 * Z == X and Y % 8 == 0
    phases = [("gx", "gy"), ("gz",)] if sizes["gx"] * sizes["gy"] <= 16 else [(a,) for a in AXES]
    groups = [group_size(sizes, axes) for axes in phases] + [1]
    slots = 3
    count = 2 * SWEEPS + 1
    out = pl.pallas_call(
        functools.partial(kernel, sizes, phases, (Z, Y, X)),
        out_shape=[jax.ShapeDtypeStruct((N, X), f32)] * 2,
        in_specs=[hbm] * 3,
        out_specs=[vm] * 2,
        scratch_shapes=[
            pltpu.VMEM((count + 1, N + 2 * Y, X), f32),
            pltpu.VMEM((count + 2, N, X), f32),
            pltpu.VMEM((N + 2 * Y, X), f32),
            pltpu.VMEM((N, X), f32),
            pltpu.VMEM((N, X), f32),
            pltpu.VMEM((N, X), f32),
            pltpu.VMEM((slots, 4 * Z + Y, X), f32),
            pltpu.VMEM((slots, 2, Y, X), f32),
            pltpu.VMEM((slots, 2, 2 * Z, X), f32),
            pltpu.VMEM((slots, 2, 2 * Y, X), f32),
            pltpu.VMEM((slots, 2, 2, 8, X), f32),
            pltpu.VMEM((slots, 2, 2, Y, X), f32),
            pltpu.VMEM((slots, 2, 2, 8, X), f32),
            pltpu.VMEM((2, Y, X), f32),
            pltpu.VMEM((2, Z, X), f32),
            pltpu.VMEM((Y, X), f32),
            pltpu.VMEM((count, 8, X), f32),
            pltpu.VMEM((count, 8, X), f32),
            pltpu.VMEM((3, 8, X), f32),
        ] + [pltpu.VMEM(((groups + [1])[i], 8, X), f32) for i in range(3)] + [
            pltpu.SemaphoreType.DMA((slots, len(DIRECTIONS))),
            pltpu.SemaphoreType.DMA((slots, len(DIRECTIONS))),
            pltpu.SemaphoreType.DMA((3, max(groups))),
            pltpu.SemaphoreType.DMA((3, max(groups))),
            pltpu.SemaphoreType.DMA((3,)),
        ],
        compiler_params=pltpu.CompilerParams(
            collective_id=0, has_side_effects=True, vmem_limit_bytes=63 * 1024 * 1024),
        name="cg",
    )(flat(right_side), flat(initial), flat(kappa_sq))
    return tuple(o.reshape(Z, Y, X) for o in out)


def solution(mesh):
    spec = P("gz", "gy", "gx")
    sizes = {a: mesh.shape[a] for a in AXES}
    return jax.shard_map(functools.partial(body, sizes), mesh=mesh, in_specs=(spec,) * 3,
                         out_specs=(spec,) * 2, check_vma=False)
```

```python
import functools
import jax
import jax.numpy as jnp
from jax import lax
from jax.experimental import pallas as pl
from jax.experimental.pallas import tpu as pltpu
from jax.sharding import PartitionSpec as P

SWEEPS = 3
GROUP = 4
cheb_high = 7.2
cheb_low = 0.072
MESH = pl.DeviceIdType.MESH
AXES = ("gx", "gy", "gz")
DIRECTIONS = [(z, y, x) for z in (-1, 0, 1) for y in (-1, 0, 1) for x in (-1, 0, 1)
              if 1 <= abs(z) + abs(y) + abs(x) <= 2]


def group_size(sizes, axes):
    size = 1
    for a in axes:
        size *= sizes[a]
    return size


def rank(sizes, where, axes):
    index = 0
    for a in axes:
        index = index * sizes[a] + where[a]
    return index


def peers(sizes, me, axes):
    found = []
    for k in range(1, group_size(sizes, axes)):
        to, origin, left = {}, {}, k
        for a in reversed(axes):
            shift, left = left % sizes[a], left // sizes[a]
            to[a] = lax.rem(me[a] + shift, sizes[a])
            origin[a] = lax.rem(me[a] + sizes[a] - shift, sizes[a])
        found.append((to, origin))
    return found


def sweep_weights():
    centre = (cheb_high + cheb_low) / 2.0
    half_width = (cheb_high - cheb_low) / 2.0
    sigma = centre / half_width
    old = 1.0 / sigma
    weights = []
    for _ in range(SWEEPS - 1):
        new = 1.0 / (2.0 * sigma - old)
        weights.append((new * old, 2.0 * new / half_width))
        old = new
    return 1.0 / centre, weights


def kernel(sizes, phases, shape, b_hbm, x0_hbm, kap_hbm, x_ref, r_ref,
           v_ref, e_ref, u_ref, t_ref, c_ref, d_ref,
           send, xhalo, yhalo, zhalo, zyhalo, zxhalo, yxhalo, cz_ref, cy_ref, cx_ref,
           sums_s, sums_v, part, gather_a, gather_b, gather_c,
           send_sem, recv_sem, red_send, red_recv, in_sem):
    Z, Y, X = shape
    N = Z * Y
    me = {a: lax.axis_index(a) for a in AXES}
    inv_centre, weights = sweep_weights()
    inv36 = 1.0 / 36.0
    half = SWEEPS
    last_q = 2 * half
    zero_slot = last_q + 2

    loads = [pltpu.make_async_copy(kap_hbm, c_ref, in_sem.at[0]),
             pltpu.make_async_copy(x0_hbm, v_ref.at[0, pl.ds(Y, N)], in_sem.at[1]),
             pltpu.make_async_copy(b_hbm, e_ref.at[0], in_sem.at[2])]
    for load in loads:
        load.start()

    for halo in (xhalo, yhalo, zhalo, zyhalo, zxhalo, yxhalo):
        halo[...] = jnp.zeros_like(halo)

    other_x = sizes["gx"] == 2

    def offset(d):
        to = {a: me[a] + s for a, s in zip(("gz", "gy", "gx"), d) if s}
        if other_x and d[2]:
            to["gx"] = 1 - me["gx"]
        return to

    def has(d):
        cond = None
        for a, s in zip(("gz", "gy", "gx"), d):
            if s and not (other_x and a == "gx"):
                one = me[a] > 0 if s < 0 else me[a] < sizes[a] - 1
                cond = one if cond is None else cond & one
        return cond

    def when(cond, fn):
        if cond is None:
            fn()
        else:
            pl.when(cond)(fn)

    DIRS = [d for d in DIRECTIONS
            if all(s == 0 or sizes[a] > 1 for a, s in zip(("gz", "gy", "gx"), d))
            and not (other_x and d[2] < 0)]

    def reverse(d):
        return (-d[0], -d[1], d[2] if other_x else -d[2])

    barrier = pltpu.get_barrier_semaphore()
    count = 0
    for d in DIRS:
        cond = has(d)

        def greet(d=d):
            pl.semaphore_signal(barrier, inc=1, device_id=offset(d), device_id_type=MESH)
        when(cond, greet)
        count = count + (1 if cond is None else jnp.where(cond, 1, 0))
    for axes in phases:
        for peer in peers(sizes, me, axes):
            pl.semaphore_signal(barrier, inc=1, device_id=peer[0], device_id_type=MESH)
            count = count + 1

    guard = jnp.zeros((Y, X), jnp.float32)
    for j in range(last_q + 2):
        v_ref[j, 0:Y, :] = guard
        v_ref[j, Y + N:2 * Y + N, :] = guard
    u_ref[0:Y, :] = guard
    u_ref[Y + N:2 * Y + N, :] = guard
    for k in range(Z):
        e_ref[zero_slot, k * Y:(k + 1) * Y, :] = guard
        d_ref[k * Y:(k + 1) * Y, :] = guard

    lane = lax.broadcasted_iota(jnp.int32, (Y, X), 1)
    row = lax.broadcasted_iota(jnp.int32, (Y, X), 0)
    quarter, place = lane // 4, lane % 4
    left_half = place < 2
    first_x, last_x = lane == 0, lane == X - 1
    edge_x = first_x | last_x
    first_y, last_y = row == 0, row == Y - 1
    lane_z = lax.broadcasted_iota(jnp.int32, (Z, X), 1)
    row_z = lax.broadcasted_iota(jnp.int32, (Z, X), 0)

    at_lo, at_x, at_hi = Z, 2 * Z, 2 * Z + Y

    def pack_y(slot, src, off):
        for at, y in ((0, 1), (at_lo, 0), (at_hi, Y - 1), (at_hi + Z, Y - 2)):
            send[slot, at:at + Z, :] = src[pl.ds(off + y, Z, stride=Y), :]

    def pack_x(slot, src, off):
        acc = jnp.zeros((Y, X), jnp.float32)
        for k in range(Z):
            v = src[off + k * Y:off + (k + 1) * Y, :]
            acc = jnp.where(quarter == k, pltpu.roll(v, (2 + 4 * k) % X, 1), acc)
        send[slot, at_x:at_x + Y, :] = acc

    def source_of(d, slot, src, off):
        dz, dy, dx = d
        out = send.at[slot]
        if dx:
            if dy == 0:
                return out.at[pl.ds(at_x, Y)]
            return out.at[pl.ds(at_x if dy < 0 else at_x + Y - 8, 8)]
        if dy and dz:
            return out.at[pl.ds((at_lo if dy < 0 else at_hi) + (0 if dz < 0 else Z - 8), 8)]
        if dy:
            return out.at[pl.ds(0 if dy < 0 else at_hi, 2 * Z)]
        return src.at[pl.ds(off if dz < 0 else off + N - 2 * Y, 2 * Y)]

    def halo_of(d, slot, side_x):
        sz, sy = (0 if s > 0 else 1 for s in d[:2])
        sx = side_x if other_x else (0 if d[2] > 0 else 1)
        dz, dy, dx = d
        if dx and dy:
            return yxhalo.at[slot, sy, sx]
        if dx and dz:
            return zxhalo.at[slot, sz, sx]
        if dx:
            return xhalo.at[slot, sx]
        if dy and dz:
            return zyhalo.at[slot, sz, sy]
        return yhalo.at[slot, sy] if dy else zhalo.at[slot, sz]

    def copy_to(d, slot, src, off):
        i = DIRECTIONS.index(d)
        return pltpu.make_async_remote_copy(
            src_ref=source_of(d, slot, src, off), dst_ref=halo_of(d, slot, me["gx"]),
            send_sem=send_sem.at[slot, i], recv_sem=recv_sem.at[slot, i],
            device_id=offset(d), device_id_type=MESH)

    def copy_from(d, slot, src, off):
        back = reverse(d)
        i = DIRECTIONS.index(back)
        return pltpu.make_async_remote_copy(
            src_ref=source_of(back, slot, src, off), dst_ref=halo_of(back, slot, 1 - me["gx"]),
            send_sem=send_sem.at[slot, i], recv_sem=recv_sem.at[slot, i],
            device_id=offset(d), device_id_type=MESH)

    def start_all(slot, src, off, packed_x=False, edges=True):
        def go(want):
            for d in DIRS:
                if want(d) and (edges or sum(1 for s in d if s) == 1):
                    when(has(d), lambda d=d: copy_to(d, slot, src, off).start())

        if packed_x:
            go(lambda d: d[2] != 0 and d[1] == 0)
        pack_y(slot, src, off)
        if packed_x:
            go(lambda d: d[2] != 0 and d[1] != 0)
        go(lambda d: d[0] != 0 and d[1] != 0 and d[2] == 0)
        go(lambda d: d[1] != 0 and d[0] == 0 and d[2] == 0)
        go(lambda d: d[0] != 0 and d[1] == 0 and d[2] == 0)
        if not packed_x:
            pack_x(slot, src, off)
            go(lambda d: d[2] != 0)

    def finish(edges, slot, src, off):
        for d in DIRS:
            if (sum(1 for s in d if s) > 1) != edges:
                continue

            def done(d=d):
                copy_from(d, slot, src, off).wait_recv()
                copy_to(d, slot, src, off).wait_send()
            when(has(d), done)

    def faces(slot):
        z1 = [zhalo[slot, 0, Y:2 * Y, :], zhalo[slot, 1, 0:Y, :]]
        y1 = [yhalo[slot, 0, 0:Z, :], yhalo[slot, 1, Z:2 * Z, :]]
        x1 = jnp.where(left_half, xhalo[slot, 0], xhalo[slot, 1])
        return z1, y1, x1

    def pairs_of(columns):
        return jnp.where(place[0:columns.shape[0]] == 2,
                         pltpu.roll(columns, 1, 1), pltpu.roll(columns, X - 1, 1))

    def along_x(v, lanes):
        return (jnp.where(lanes == 0, 0.0, pltpu.roll(v, 1, 1))
                + jnp.where(lanes == X - 1, 0.0, pltpu.roll(v, X - 1, 1)))

    exists = {a: [jnp.where(me[a] > 0, 1.0, 0.0).astype(jnp.float32),
                  jnp.where(me[a] < sizes[a] - 1, 1.0, 0.0).astype(jnp.float32)] for a in AXES}

    def along_y(f):
        return (jnp.where(first_y, 0.0, pltpu.roll(f, 1, 0))
                + jnp.where(last_y, 0.0, pltpu.roll(f, Y - 1, 0)))

    def k_inner(src, dst, dst_off):
        for base in range(0, Z, GROUP):
            done = []
            for k in range(base, min(base + GROUP, Z)):
                i = Y + k * Y
                v = src[i:i + Y, :]
                total = src[i - Y:i, :] + src[i + Y:i + 2 * Y, :] + along_x(v, lane)
                total = total + jnp.where(first_y, 0.0, src[i - 1:i - 1 + Y, :])
                total = total + jnp.where(last_y, 0.0, src[i + 1:i + 1 + Y, :])
                done.append((k, c_ref[k * Y:(k + 1) * Y, :] * v - total))
            for k, value in done:
                dst[dst_off + k * Y:dst_off + (k + 1) * Y, :] = value

    def k_edges(slot, v, off):
        z1, y1, x1 = faces(slot)
        z2 = [zhalo[slot, 0, 0:Y, :], zhalo[slot, 1, Y:2 * Y, :]]
        y2 = [yhalo[slot, 0, Z:2 * Z, :], yhalo[slot, 1, 0:Z, :]]
        zx = [pairs_of(jnp.where(left_half, zxhalo[slot, s, 0], zxhalo[slot, s, 1])) for s in (0, 1)]
        yx = [pairs_of(jnp.where(left_half[0:8], yxhalo[slot, s, 0], yxhalo[slot, s, 1]))
              for s in (0, 1)]
        zy = [[zyhalo[slot, sz, sy, r:r + 1, :] for sy in (0, 1)] for sz, r in ((0, 7), (1, 0))]
        for s, k, inward in ((0, 0, 1), (1, Z - 1, Z - 2)):
            f = z1[s]
            rows = slice(k * Y, (k + 1) * Y)
            own = v[off + k * Y:off + (k + 1) * Y, :] * exists["gz"][s]
            side = along_x(f, lane) + along_y(f)
            t_ref[rows, :] = t_ref[rows, :] + (z2[s] + own + 2.0 * side - cz_ref[s] * f)
            rows = slice(inward * Y, (inward + 1) * Y)
            t_ref[rows, :] = t_ref[rows, :] + f
        for s, y, inward, at in ((0, 0, 1, at_lo), (1, Y - 1, Y - 2, at_hi)):
            f = y1[s]
            rows = pl.ds(y, Z, stride=Y)
            own = send[slot, at:at + Z, :] * exists["gy"][s]
            side = along_x(f, lane_z)
            side = side + jnp.where(row_z == 0, zy[0][s], pltpu.roll(f, 1, 0))
            side = side + jnp.where(row_z == Z - 1, zy[1][s], pltpu.roll(f, Z - 1, 0))
            t_ref[rows, :] = t_ref[rows, :] + (y2[s] + own + 2.0 * side - cy_ref[s] * f)
            rows = pl.ds(inward, Z, stride=Y)
            t_ref[rows, :] = t_ref[rows, :] + f
        f = pairs_of(x1)
        x2 = jnp.where(place == 2, pltpu.roll(x1, 2, 1), pltpu.roll(x1, X - 2, 1))
        own = send[slot, at_x:at_x + Y, :] * jnp.where(place == 2, exists["gx"][0], exists["gx"][1])
        side = jnp.where(first_y, yx[0][7:8, :], pltpu.roll(f, 1, 0))
        side = side + jnp.where(last_y, yx[1][0:1, :], pltpu.roll(f, Y - 1, 0))
        side = side + jnp.where(lane < 4, pltpu.roll(zx[0], 4, 1), pltpu.roll(f, 4, 1))
        side = side + jnp.where(lane >= X - 4, pltpu.roll(zx[1], X - 4, 1), pltpu.roll(f, X - 4, 1))
        edge = x2 + own + 2.0 * side - cx_ref[...] * f
        return jnp.where(place == 3, pltpu.roll(f, 1, 1),
                         jnp.where(place == 0, pltpu.roll(f, X - 1, 1), edge))

    two_x = (lane < 2) | (lane >= X - 2)

    loads[0].wait()
    pl.semaphore_wait(barrier, count)
    start_all(2, c_ref, 0, edges=False)
    loads[1].wait()
    start_all(0, v_ref.at[0], Y)
    loads[2].wait()
    finish(False, 2, c_ref, 0)
    kz, ky, kx = faces(2)
    for s, k, at in ((0, 0, at_lo), (1, Z - 1, at_hi)):
        cz_ref[s] = 12.0 + kz[s] + c_ref[k * Y:(k + 1) * Y, :]
        cy_ref[s] = 12.0 + ky[s] + send[2, at:at + Z, :]
    cx_ref[...] = 12.0 + pairs_of(kx) + send[2, at_x:at_x + Y, :]
    for k in range(Z):
        rows = slice(k * Y, (k + 1) * Y)
        c_ref[rows, :] = 6.0 + c_ref[rows, :]

    gathers = (gather_a, gather_b, gather_c)

    def red_start(i, value):
        part[i] = value
        gathers[i][pl.ds(rank(sizes, me, phases[i]), 1)] = value[None]
        for k, (peer, _) in enumerate(peers(sizes, me, phases[i])):
            pltpu.make_async_remote_copy(
                src_ref=part.at[i], dst_ref=gathers[i].at[rank(sizes, me, phases[i])],
                send_sem=red_send.at[i, k], recv_sem=red_recv.at[i, k],
                device_id=peer, device_id_type=MESH).start()

    def red_finish(i):
        for k, (peer, origin) in enumerate(peers(sizes, me, phases[i])):
            copy = pltpu.make_async_remote_copy(
                src_ref=part.at[i], dst_ref=gathers[i].at[rank(sizes, origin, phases[i])],
                send_sem=red_send.at[i, k], recv_sem=red_recv.at[i, k],
                device_id=peer, device_id_type=MESH)
            copy.wait_recv()
            copy.wait_send()
        total = gathers[i][0]
        for j in range(1, group_size(sizes, phases[i])):
            total = total + gathers[i][j]
        return total

    def red_first():
        rows8 = lax.broadcasted_iota(jnp.int32, (8, X), 0)
        mine = jnp.zeros((8, X), jnp.float32)
        for j, value in enumerate((sums_s[half - 1], sums_v[half], sums_s[last_q - 1], sums_v[last_q])):
            mine = jnp.where(rows8 == j, jnp.sum(value, axis=0, keepdims=True), mine)
        red_start(0, mine)

    def q_body(q, carry):
        phase = lax.rem(q, half)
        sweep = jnp.minimum(phase, 1)
        source = sweep * (1 + half * (q // half)) + (1 - sweep) * zero_slot * ((q + last_q - 1) // last_q)
        sign = jnp.where((sweep == 0) & (q > 0), -1.0, 1.0).astype(jnp.float32)
        old, new, keep = jnp.float32(0.0), sign * jnp.float32(inv_centre), jnp.float32(0.0)
        for j, (wo, wn) in enumerate(weights):
            old = jnp.where(phase == j + 1, jnp.float32(wo), old)
            new = jnp.where(phase == j + 1, jnp.float32(wn), new)
            keep = jnp.where(phase == j + 1, jnp.float32(1.0), keep)
        v = v_ref.at[q]
        v_new = v_ref.at[q + 1]
        zero8 = jnp.zeros((8, X), jnp.float32)
        acc = {"s": zero8, "v": zero8, "x": jnp.zeros((Y, X), jnp.float32)}

        def fold(name, value):
            for j in range(0, Y, 8):
                acc[name] = acc[name] + value[j:j + 8]

        def post_t(k, t):
            rows = slice(k * Y, (k + 1) * Y)
            vrows = slice(Y + k * Y, 2 * Y + k * Y)
            t = t * inv36
            src = e_ref[source, rows, :]
            defect = src - t
            upd = old * d_ref[rows, :] + new * defect
            was = v[vrows, :]
            z = keep * was + upd
            fold("s", src * z)
            fold("v", was * t)
            acc["x"] = jnp.where(quarter == k, pltpu.roll(z, (2 + 4 * k) % X, 1), acc["x"])

            def store():
                e_ref[q + 1, rows, :] = sign * defect
                d_ref[rows, :] = upd
                v_new[vrows, :] = z
            return store

        slot = lax.rem(q, 2)
        k_inner(v, u_ref, Y)
        k_inner(u_ref, t_ref, 0)
        finish(False, slot, v, Y)
        finish(True, slot, v, Y)
        columns = k_edges(slot, v, Y)
        for base in range(0, Z, GROUP):
            stores = []
            for k in range(base, min(base + GROUP, Z)):
                fix = jnp.where(two_x, pltpu.roll(columns, (2 * X - 2 - 4 * k) % X, 1), 0.0)
                stores.append(post_t(k, t_ref[k * Y:(k + 1) * Y, :] + fix))
            for store in stores:
                store()
        send[1 - slot, at_x:at_x + Y, :] = acc["x"]
        pl.when(q < last_q)(lambda: start_all(1 - slot, v_new, Y, packed_x=True))
        sums_s[q] = acc["s"]
        sums_v[q] = acc["v"]
        return carry

    lax.fori_loop(0, last_q + 1, q_body, 0)

    red_first()
    total = red_finish(0)
    for i in range(1, len(phases)):
        red_start(i, total)
        total = red_finish(i)
    totals = jnp.sum(total, axis=1, keepdims=True)
    e0, g1, g2 = totals[0:1], totals[1:2], totals[2:3]
    g3 = totals[3:4]
    alpha = e0 / g1
    e1 = e0 - 2.0 * alpha * g1 + alpha * alpha * g2
    keep = 1.0 + e1 / e0
    den = keep * keep * g1 - 2.0 * keep * alpha * g2 + alpha * alpha * g3
    alpha1 = e1 / den
    p = alpha + alpha1 * keep
    q = alpha1 * alpha
    for k in range(Z):
        rows = slice(k * Y, (k + 1) * Y)
        vrows = slice(Y + k * Y, 2 * Y + k * Y)
        x_ref[rows, :] = v_ref[0, vrows, :] + p * v_ref[half, vrows, :] - q * v_ref[last_q, vrows, :]
        r_ref[rows, :] = e_ref[1, rows, :] - p * e_ref[half + 1, rows, :] + q * e_ref[last_q + 1, rows, :]


def body(sizes, right_side, initial, kappa_sq):
    Z, Y, X = right_side.shape
    N = Z * Y
    f32 = jnp.float32
    flat = lambda a: a.reshape(N, X)
    vm = pl.BlockSpec(memory_space=pltpu.VMEM)
    hbm = pl.BlockSpec(memory_space=pltpu.HBM)
    assert 4 * Z == X and Y % 8 == 0
    phases = [("gx", "gy"), ("gz",)] if sizes["gx"] * sizes["gy"] <= 16 else [(a,) for a in AXES]
    groups = [group_size(sizes, axes) for axes in phases] + [1]
    slots = 3
    count = 2 * SWEEPS + 1
    out = pl.pallas_call(
        functools.partial(kernel, sizes, phases, (Z, Y, X)),
        out_shape=[jax.ShapeDtypeStruct((N, X), f32)] * 2,
        in_specs=[hbm] * 3,
        out_specs=[vm] * 2,
        scratch_shapes=[
            pltpu.VMEM((count + 1, N + 2 * Y, X), f32),
            pltpu.VMEM((count + 2, N, X), f32),
            pltpu.VMEM((N + 2 * Y, X), f32),
            pltpu.VMEM((N, X), f32),
            pltpu.VMEM((N, X), f32),
            pltpu.VMEM((N, X), f32),
            pltpu.VMEM((slots, 4 * Z + Y, X), f32),
            pltpu.VMEM((slots, 2, Y, X), f32),
            pltpu.VMEM((slots, 2, 2 * Z, X), f32),
            pltpu.VMEM((slots, 2, 2 * Y, X), f32),
            pltpu.VMEM((slots, 2, 2, 8, X), f32),
            pltpu.VMEM((slots, 2, 2, Y, X), f32),
            pltpu.VMEM((slots, 2, 2, 8, X), f32),
            pltpu.VMEM((2, Y, X), f32),
            pltpu.VMEM((2, Z, X), f32),
            pltpu.VMEM((Y, X), f32),
            pltpu.VMEM((count, 8, X), f32),
            pltpu.VMEM((count, 8, X), f32),
            pltpu.VMEM((3, 8, X), f32),
        ] + [pltpu.VMEM(((groups + [1])[i], 8, X), f32) for i in range(3)] + [
            pltpu.SemaphoreType.DMA((slots, len(DIRECTIONS))),
            pltpu.SemaphoreType.DMA((slots, len(DIRECTIONS))),
            pltpu.SemaphoreType.DMA((3, max(groups))),
            pltpu.SemaphoreType.DMA((3, max(groups))),
            pltpu.SemaphoreType.DMA((3,)),
        ],
        compiler_params=pltpu.CompilerParams(
            collective_id=0, has_side_effects=True, vmem_limit_bytes=63 * 1024 * 1024),
        name="cg",
    )(flat(right_side), flat(initial), flat(kappa_sq))
    return tuple(o.reshape(Z, Y, X) for o in out)


def solution(mesh):
    spec = P("gz", "gy", "gx")
    sizes = {a: mesh.shape[a] for a in AXES}
    return jax.shard_map(functools.partial(body, sizes), mesh=mesh, in_specs=(spec,) * 3,
                         out_specs=(spec,) * 2, check_vma=False)
```
